128 devices in a mesh: group: 8 (over z, x_hi), local: 16 (over x_lo, y, core).
Axes of the slice: x: 4 (x_hi: 2, x_lo: 2; x = x_hi * 2 + x_lo), y: 4, z: 4, core: 2. Of those that a mesh axis runs over, the one named last changes fastest.
Arguments:
- features: bfloat16 [262144, 512], P(('group', 'local')), may hold values from -6 to 6
- weight: bfloat16 [512, 512], replicated, may hold values from -0.25 to 0.25
- cotangent: bfloat16 [262144, 512], P(('group', 'local')), may hold values from -6 to 6
- tile_vals: bfloat16 [32768, 128, 128], P(('group', 'local')), may hold values from -0.125 to 0.125
- tile_rows: int32 [32768], P(('group', 'local')), may hold values from 0 to 15
- tile_cols: int32 [32768], P(('group', 'local')), may hold values from 0 to 47
- send_rows: int32 [128, 128, 32], P(('group', 'local')), may hold values from 0 to 2047, as said below
- counts: int32 [128, 128], P(('group', 'local')), may hold values from 1 to 32, as said below
Outputs:
- activated: bfloat16 [262144, 512], P(('group', 'local'))
- feature_grad: bfloat16 [262144, 512], P(('group', 'local'))
- weight_grad: float32 [512, 512], replicated
The draws below stay inside these ranges and needn't reach their ends.
Inputs may be any that keep to these rules, and one draw needn't show every extreme that they name: Each list send_rows[s, d] holds 32 distinct local row numbers of device s. `counts`: some destinations are busy: every source sends them 32 rows; at least one such destination exists.
All inputs are finite; a program needn't handle non-finite values.
Results may differ from the reference program's by a relative error of at most 0.006.
Values may be sent and summed in bfloat16 or wider, within the bound.
A program may use at most 192 MiB of HBM per device.

```python
import jax
import jax.numpy as jnp
from jax import lax

WIDTH = 512
TILE = 128
ROWS_DEV = 2048
TILES_DEV = 256
SLOTS = 32
ROW_BLOCKS = 16
COL_BLOCKS = 48
NODES = 262144
ALL_TILES = 32768
DEVICES = 128


def draw_send_rows(key, part):
    key = jax.random.fold_in(key, 11)
    scores = jax.random.randint(key, (DEVICES, DEVICES, ROWS_DEV), 0, 2 ** 19)
    distinct = scores * ROWS_DEV + jnp.arange(ROWS_DEV, dtype=jnp.int32)
    chosen_values, chosen = lax.top_k(distinct, SLOTS)
    return (chosen_values % ROWS_DEV).astype(jnp.int32)


def draw_counts(key, part):
    key = jax.random.fold_in(key, 23)
    key_busy, key_pick, key_count = jax.random.split(key, 3)
    busy = jax.random.randint(key_busy, (DEVICES,), 0, 8) == 0
    forced = jax.random.randint(key_pick, (), 0, DEVICES)
    busy = busy | (jnp.arange(DEVICES) == forced)
    quiet = jax.random.randint(key_count, (DEVICES, DEVICES), 1, SLOTS // 2 + 1)
    return jnp.where(busy[None, :], SLOTS, quiet).astype(jnp.int32)


def set_ends(values, stream_key, low, largest):
    longest = values.shape.index(max(values.shape))
    spots = []
    for shift in (0, 1):
        where = [jax.random.randint(jax.random.fold_in(stream_key, axis), (), 0, length) for axis, length in enumerate(values.shape)]
        where[longest] = (where[longest] + shift) % values.shape[longest]
        spots.append(tuple(where))
    return values.at[spots[0]].set(low).at[spots[1]].set(largest)


def block_levels(rng, dims, pieces, low, high):
    loudness, own = 1.0, jax.random.fold_in(rng, 6)
    for dim, blocks in pieces:
        steps = jnp.exp(jax.random.uniform(jax.random.fold_in(own, dim), (blocks,), jnp.float32, low / len(pieces), high / len(pieces)))
        loudness = loudness * jnp.repeat(steps, dims[dim] // blocks).reshape([-1 if axis == dim else 1 for axis in range(len(dims))])
    return loudness


def centred(stream_key, dims, scale, most, cuts=(), kind=jnp.bfloat16):
    loudness = block_levels(stream_key, dims, cuts, -0.22, 0.18) if cuts else 1.0
    array = jax.random.normal(stream_key, dims, jnp.float32) * scale * loudness
    return jnp.minimum(jnp.maximum(array, -most), most).astype(kind)


def setup_inputs(seed: int = 0) -> dict:
    arg_keys = jax.random.split(jax.random.key(seed), 9)
    features = centred(arg_keys[0], (NODES, WIDTH), 1.0, 6.0, ((0, 128),))
    weight = centred(arg_keys[1], (WIDTH, WIDTH), WIDTH ** -0.5, 0.25)
    cotangent = centred(arg_keys[2], (NODES, WIDTH), 1.0, 6.0, ((0, 128),))
    tile_vals = centred(arg_keys[3], (ALL_TILES, TILE, TILE), (TILES_DEV * TILE // ROW_BLOCKS) ** -0.5, 0.125, ((0, 128),))
    tile_rows = set_ends(jax.random.randint(arg_keys[4], (ALL_TILES,), 0, ROW_BLOCKS), jax.random.fold_in(arg_keys[4], 1), 0, ROW_BLOCKS - 1).astype(jnp.int32)
    tile_cols = set_ends(jax.random.randint(arg_keys[5], (ALL_TILES,), 0, COL_BLOCKS), jax.random.fold_in(arg_keys[5], 1), 0, COL_BLOCKS - 1).astype(jnp.int32)
    send_rows = draw_send_rows(jax.random.fold_in(arg_keys[8], 71), 0)
    counts = draw_counts(jax.random.fold_in(arg_keys[8], 71), 0)
    return dict(features=features, weight=weight, cotangent=cotangent, tile_vals=tile_vals, tile_rows=tile_rows, tile_cols=tile_cols, send_rows=send_rows, counts=counts)


def tiles_of(tile_vals, tile_rows, tile_cols, device):
    start = device * TILES_DEV
    values = lax.dynamic_slice_in_dim(tile_vals, start, TILES_DEV, 0)
    rows_of = lax.dynamic_slice_in_dim(tile_rows, start, TILES_DEV, 0)
    cols_of = lax.dynamic_slice_in_dim(tile_cols, start, TILES_DEV, 0)
    return values, rows_of, cols_of


def reference(features, weight, cotangent, tile_vals, tile_rows, tile_cols, send_rows, counts):
    slot_ids = jnp.arange(SLOTS).astype(jnp.int32)
    sources = jnp.arange(DEVICES).astype(jnp.int32)

    def remote_index(device):
        indices = sources[:, None] * ROWS_DEV + send_rows[:, device, :]
        live_slots = slot_ids[None, :] < counts[:, device][:, None]
        return indices, live_slots

    def forward(device):
        owned = lax.dynamic_slice_in_dim(features, device * ROWS_DEV, ROWS_DEV, 0)
        indices, live_slots = remote_index(device)
        remote = jnp.where(live_slots[..., None], features[indices], jnp.zeros((), features.dtype))
        extended = jnp.concatenate([owned, remote.reshape(-1, WIDTH)], axis=0).reshape(COL_BLOCKS, TILE, WIDTH)
        values, rows_of, cols_of = tiles_of(tile_vals, tile_rows, tile_cols, device)
        product = jnp.einsum('tij,tjf->tif', values.astype(jnp.float32), extended[cols_of].astype(jnp.float32),
                             precision=lax.Precision.HIGHEST)
        summed = jax.ops.segment_sum(product, rows_of, num_segments=ROW_BLOCKS)
        return summed.reshape(ROWS_DEV, WIDTH).astype(jnp.bfloat16)

    hidden = lax.map(forward, sources).reshape(NODES, WIDTH)
    preact = jnp.dot(hidden, weight, preferred_element_type=jnp.float32)
    gate = jax.nn.sigmoid(preact)
    activated = (preact * gate).astype(jnp.bfloat16)
    slope = (cotangent.astype(jnp.float32) * gate * (1.0 + preact * (1.0 - gate))).astype(jnp.bfloat16)
    weight_grad = jnp.dot(hidden.T, slope, preferred_element_type=jnp.float32)
    hidden_grad = jnp.dot(slope, weight.T, preferred_element_type=jnp.float32).astype(jnp.bfloat16)

    def backward(total, device):
        values, rows_of, cols_of = tiles_of(tile_vals, tile_rows, tile_cols, device)
        block_grad = lax.dynamic_slice_in_dim(hidden_grad, device * ROWS_DEV, ROWS_DEV, 0).reshape(ROW_BLOCKS, TILE, WIDTH)
        product = jnp.einsum('tji,tjf->tif', values.astype(jnp.float32), block_grad[rows_of].astype(jnp.float32),
                             precision=lax.Precision.HIGHEST)
        spread = jax.ops.segment_sum(product, cols_of, num_segments=COL_BLOCKS).reshape(-1, WIDTH)
        owned = spread[:ROWS_DEV]
        indices, live_slots = remote_index(device)
        returned = jnp.where(live_slots[..., None], spread[ROWS_DEV:].reshape(DEVICES, SLOTS, WIDTH), jnp.float32(0.0))
        current = lax.dynamic_slice_in_dim(total, device * ROWS_DEV, ROWS_DEV, 0)
        total = lax.dynamic_update_slice_in_dim(total, current + owned, device * ROWS_DEV, 0)
        total = total.at[indices.reshape(-1)].add(returned.reshape(-1, WIDTH))
        return total, None

    total, unused = lax.scan(backward, jnp.zeros((NODES, WIDTH), jnp.float32), sources)
    return activated, total.astype(jnp.bfloat16), weight_grad
```

```python
import functools

import jax
import jax.numpy as jnp
from jax import lax
from jax.experimental import pallas as pl
from jax.experimental.pallas import tpu as pltpu
from jax.sharding import PartitionSpec as P

MESH = pl.DeviceIdType.MESH
F32 = jnp.float32
BF16 = jnp.bfloat16
VMEM_LIMIT = 60 * 1024 * 1024


def place(groups, locals_):
    g = lax.axis_index("group")
    l = lax.axis_index("local")
    return g, l, g * locals_ + l


def greet_all(groups, locals_):
    g, l, me = place(groups, locals_)
    barrier = pltpu.get_barrier_semaphore()

    @pl.loop(1, groups * locals_)
    def _(k):
        peer = lax.rem(me + k, groups * locals_)
        pl.semaphore_signal(
            barrier,
            inc=1,
            device_id=(lax.div(peer, locals_), lax.rem(peer, locals_)),
            device_id_type=MESH,
        )

    pl.semaphore_wait(barrier, groups * locals_ - 1)


def wait_rows(ref, rows, sem):
    view = ref.at[pl.ds(0, rows)]
    pltpu.make_async_copy(view, view, sem).wait()


def exchange_kernel(groups, locals_, slots, feat, idx, arrived, outgoing, send_sem, recv_sem, own_sem):
    g, l, me = place(groups, locals_)
    batch = locals_ * slots
    rows_own = feat.shape[0]
    greet_all(groups, locals_)

    def send_group(step, first):
        dest_g = lax.rem(g + groups - step, groups)
        base = dest_g * batch
        picks = idx[pl.ds(base, batch), :]
        cols = lax.broadcasted_iota(jnp.int32, (batch, rows_own), 1)
        onehot = (picks == cols).astype(F32).astype(BF16)
        rows = jnp.dot(onehot, feat[...], preferred_element_type=F32)
        outgoing[pl.ds(base, batch), :] = rows.astype(BF16)

        @pl.loop(1 if first else 0, locals_)
        def _(i):
            dest_l = lax.rem(l + i, locals_)
            pltpu.make_async_remote_copy(
                src_ref=outgoing.at[pl.ds(base + dest_l * slots, slots)],
                dst_ref=arrived.at[pl.ds(me * slots, slots)],
                send_sem=send_sem.at[step],
                recv_sem=recv_sem.at[step],
                device_id=(dest_g, dest_l),
                device_id_type=MESH,
            ).start()

    send_group(0, True)
    own = pltpu.make_async_copy(
        outgoing.at[pl.ds(me * slots, slots)], arrived.at[pl.ds(me * slots, slots)], own_sem
    )
    own.start()

    @pl.loop(1, groups)
    def _(step):
        send_group(step, False)

    own.wait()
    wait_rows(outgoing, batch - slots, send_sem.at[0])
    wait_rows(arrived, batch - slots, recv_sem.at[0])

    @pl.loop(1, groups)
    def _(step):
        wait_rows(outgoing, batch, send_sem.at[step])
        wait_rows(arrived, batch, recv_sem.at[step])


def layer_kernel(
    order_f, start_f, order_b, start_b,
    feat, arrived, vals, weight, cot,
    activated, wgrad, remote, owned,
    vbuf, xbuf, cotbuf, wbuf, actbuf, hidden, hgrad, slope, acc, rembuf, ownbuf, sems,
):
    tiles, edge, _ = vals.shape
    rows_own, width = feat.shape
    row_blocks = rows_own // edge
    col_blocks = xbuf.shape[0] // edge
    loads = [
        pltpu.make_async_copy(feat, xbuf.at[pl.ds(0, rows_own)], sems.at[0]),
        pltpu.make_async_copy(arrived, xbuf.at[pl.ds(rows_own, xbuf.shape[0] - rows_own)], sems.at[1]),
        pltpu.make_async_copy(vals, vbuf.at[pl.ds(0, tiles)], sems.at[2]),
        pltpu.make_async_copy(cot, cotbuf, sems.at[3]),
        pltpu.make_async_copy(weight, wbuf, sems.at[4]),
    ]
    for load in loads:
        load.start()
    vbuf[tiles] = jnp.zeros((edge, edge), BF16)
    for load in loads:
        load.wait()

    depth = 4

    def tile_of(order, at, end):
        return jnp.where(at < end, order[jnp.minimum(at, tiles - 1)], tiles)

    @pl.loop(0, row_blocks)
    def _(r):
        begin, end = start_f[r], start_f[r + 1]
        acc[...] = jnp.zeros_like(acc)

        @pl.loop(0, lax.div(end - begin + depth - 1, depth))
        def _(q):
            left, right = [], []
            for k in range(depth):
                at = begin + q * depth + k
                t = tile_of(order_f, at, end)
                packed = order_f[tiles + jnp.minimum(at, tiles - 1)]
                left.append(vbuf[t])
                right.append(xbuf[pl.ds(pl.multiple_of(packed * edge, edge), edge), :])
            acc[...] += jnp.dot(
                jnp.concatenate(left, axis=1),
                jnp.concatenate(right, axis=0),
                preferred_element_type=F32,
            )

        hidden[pl.ds(pl.multiple_of(r * edge, edge), edge), :] = acc[...].astype(BF16)

    wgrad[...] = jnp.zeros_like(wgrad)
    band = 512

    @pl.loop(0, rows_own // band)
    def _(b):
        at = pl.ds(pl.multiple_of(b * band, band), band)
        h = hidden[at, :]
        pre = jnp.dot(h, wbuf[...], preferred_element_type=F32)
        gate = jax.nn.sigmoid(pre)
        actbuf[at, :] = (pre * gate).astype(BF16)
        s = (cotbuf[at, :].astype(F32) * gate * (1.0 + pre * (1.0 - gate))).astype(BF16)
        hgrad[at, :] = lax.dot_general(
            s, wbuf[...], (((1,), (1,)), ((), ())), preferred_element_type=F32
        ).astype(BF16)
        wgrad[...] += lax.dot_general(h, s, (((0,), (0,)), ((), ())), preferred_element_type=F32)

    save_act = pltpu.make_async_copy(actbuf, activated, sems.at[0])
    save_act.start()

    def spread_block(c):
        begin, end = start_b[c], start_b[c + 1]
        acc[...] = jnp.zeros_like(acc)

        @pl.loop(0, lax.div(end - begin + 1, 2))
        def _(q):
            left, right = [], []
            for k in range(2):
                at = begin + q * 2 + k
                t = tile_of(order_b, at, end)
                r = order_b[tiles + jnp.minimum(at, tiles - 1)]
                left.append(vbuf[t])
                right.append(hgrad[pl.ds(pl.multiple_of(r * edge, edge), edge), :])
            acc[...] += lax.dot_general(
                jnp.concatenate(left, axis=0),
                jnp.concatenate(right, axis=0),
                (((0,), (0,)), ((), ())),
                preferred_element_type=F32,
            )

    @pl.loop(row_blocks, col_blocks)
    def _(c):
        spread_block(c)
        rembuf[pl.ds(pl.multiple_of((c - row_blocks) * edge, edge), edge), :] = acc[...].astype(BF16)

    save_rem = pltpu.make_async_copy(rembuf, remote, sems.at[1])
    save_rem.start()

    @pl.loop(0, row_blocks)
    def _(c):
        spread_block(c)
        ownbuf[pl.ds(pl.multiple_of(c * edge, edge), edge), :] = acc[...]

    save_own = pltpu.make_async_copy(ownbuf, owned, sems.at[2])
    save_own.start()
    save_act.wait()
    save_rem.wait()
    save_own.wait()


def return_kernel(
    groups, locals_, slots,
    remote, owned, idx, part,
    grad, wgrad,
    returned, total, wsum, sib, chunks, gathered,
    send_sem, recv_sem, own_sems, sib_send, sib_recv, rs_send, rs_recv, ag_send, ag_recv,
):
    g, l, me = place(groups, locals_)
    batch = locals_ * slots
    rows_own, width = total.shape
    core = lax.rem(l, 2)
    mates = locals_ // 2
    chips = groups * mates
    chip = g * mates + lax.div(l, 2)
    half = part.shape[0] // 2
    edge_r, edge_c = chunks.shape[1:]
    across = width // edge_c

    load_own = pltpu.make_async_copy(owned, total, own_sems.at[0])
    load_own.start()
    keep = pltpu.make_async_copy(
        remote.at[pl.ds(me * slots, slots)], returned.at[pl.ds(me * slots, slots)], own_sems.at[1]
    )
    keep.start()
    greet_all(groups, locals_)

    mine = pl.multiple_of(core * half, half)
    other = pl.multiple_of((1 - core) * half, half)
    sibling = (g, l + 1 - 2 * core)
    swap = pltpu.make_async_remote_copy(
        src_ref=part.at[pl.ds(other, half)],
        dst_ref=sib,
        send_sem=sib_send.at[0],
        recv_sem=sib_recv.at[0],
        device_id=sibling,
        device_id_type=MESH,
    )
    swap.start()

    def send_group(step, first):
        dest_g = lax.rem(g + groups - step, groups)
        base = dest_g * batch

        @pl.loop(1 if first else 0, locals_)
        def _(i):
            dest_l = lax.rem(l + i, locals_)
            pltpu.make_async_remote_copy(
                src_ref=remote.at[pl.ds(base + dest_l * slots, slots)],
                dst_ref=returned.at[pl.ds(me * slots, slots)],
                send_sem=send_sem.at[step],
                recv_sem=recv_sem.at[step],
                device_id=(dest_g, dest_l),
                device_id_type=MESH,
            ).start()

    def spot(q):
        return lax.div(q, across) * edge_r, lax.rem(q, across) * edge_c

    def peer_of(q):
        return (lax.div(q, mates), 2 * lax.rem(q, mates) + core)

    swap.wait()
    wsum[...] = part[pl.ds(mine, half), :] + sib[...]

    @pl.loop(1, chips)
    def _(k):
        q = lax.rem(chip + k, chips)
        r0, c0 = spot(q)
        pltpu.make_async_remote_copy(
            src_ref=wsum.at[pl.ds(pl.multiple_of(r0, edge_r), edge_r), pl.ds(pl.multiple_of(c0, edge_c), edge_c)],
            dst_ref=chunks.at[chip],
            send_sem=rs_send,
            recv_sem=rs_recv,
            device_id=peer_of(q),
            device_id_type=MESH,
        ).start()

    send_group(0, True)

    @pl.loop(1, groups)
    def _(step):
        send_group(step, False)

    r0, c0 = spot(chip)
    here = (pl.ds(pl.multiple_of(r0, edge_r), edge_r), pl.ds(pl.multiple_of(c0, edge_c), edge_c))
    chunks[chip] = wsum[here[0], here[1]]
    wait_rows(chunks, chips - 1, rs_send)
    wait_rows(chunks, chips - 1, rs_recv)
    gathered[...] = jnp.sum(chunks[...], axis=0)
    there = (pl.ds(pl.multiple_of(mine + r0, edge_r), edge_r), here[1])
    wgrad[there[0], there[1]] = gathered[...]

    @pl.loop(1, chips)
    def _(k):
        q = lax.rem(chip + k, chips)
        pltpu.make_async_remote_copy(
            src_ref=gathered,
            dst_ref=wgrad.at[there[0], there[1]],
            send_sem=ag_send,
            recv_sem=ag_recv,
            device_id=peer_of(q),
            device_id_type=MESH,
        ).start()

    load_own.wait()
    keep.wait()

    def add_group(step):
        src_g = lax.rem(g + step, groups)
        base = pl.multiple_of(src_g * batch, batch)
        picks = idx[:, pl.ds(base, batch)]
        rows = returned[pl.ds(base, batch), :]
        band = 512

        @pl.loop(0, rows_own // band)
        def _(b):
            at = pl.multiple_of(b * band, band)
            ids = lax.broadcasted_iota(jnp.int32, (band, batch), 0) + at
            onehot = (ids == picks).astype(F32).astype(BF16)
            total[pl.ds(at, band), :] += jnp.dot(onehot, rows, preferred_element_type=F32)

    wait_rows(returned, batch - slots, recv_sem.at[0])
    add_group(0)

    @pl.loop(1, groups)
    def _(step):
        wait_rows(returned, batch, recv_sem.at[step])
        add_group(step)

    wait_rows(chunks, chips - 1, ag_send)
    wait_rows(chunks, chips - 1, ag_recv)
    back = pltpu.make_async_remote_copy(
        src_ref=wgrad.at[pl.ds(mine, half)],
        dst_ref=wgrad.at[pl.ds(mine, half)],
        send_sem=sib_send.at[1],
        recv_sem=sib_recv.at[1],
        device_id=sibling,
        device_id_type=MESH,
    )
    back.start()
    grad[...] = total[...].astype(BF16)
    wait_rows(returned, batch - slots, send_sem.at[0])

    @pl.loop(1, groups)
    def _(step):
        wait_rows(returned, batch, send_sem.at[step])

    back.wait()


def ordered(keys, mates, buckets):
    n = keys.shape[0]
    ids = jnp.arange(n, dtype=jnp.int32)
    full = keys * n + ids
    rank = jnp.sum((full[None, :] < full[:, None]).astype(jnp.int32), axis=1)
    hit = rank[:, None] == ids[None, :]
    order = jnp.sum(jnp.where(hit, ids[:, None], 0), axis=0)
    paired = jnp.sum(jnp.where(hit, mates[:, None], 0), axis=0)
    starts = jnp.sum((keys[None, :] < jnp.arange(buckets + 1, dtype=jnp.int32)[:, None]).astype(jnp.int32), axis=1)
    return jnp.concatenate([order, paired]), starts


def per_device(groups, locals_, features, weight, cotangent, tile_vals, tile_rows, tile_cols, send_rows, counts):
    rows_own, width = features.shape
    tiles, edge, _ = tile_vals.shape
    peers, slots = send_rows.shape[1:]
    row_blocks = rows_own // edge
    remote_rows = peers * slots
    col_blocks = (rows_own + remote_rows) // edge
    live = jnp.arange(slots, dtype=jnp.int32)[None, :] < counts[0][:, None]
    idx = jnp.where(live, send_rows[0], -1)
    any_ = pl.BlockSpec(memory_space=pl.ANY)
    vmem = pl.BlockSpec(memory_space=pltpu.VMEM)
    smem = pl.BlockSpec(memory_space=pltpu.SMEM)
    order_f, start_f = ordered(tile_rows, tile_cols, row_blocks)
    order_b, start_b = ordered(tile_cols, tile_rows, col_blocks)

    arrived = pl.pallas_call(
        functools.partial(exchange_kernel, groups, locals_, slots),
        out_shape=jax.ShapeDtypeStruct((remote_rows, width), BF16),
        in_specs=[vmem, vmem],
        out_specs=any_,
        scratch_shapes=[
            pltpu.VMEM((remote_rows, width), BF16),
            pltpu.SemaphoreType.DMA((groups,)),
            pltpu.SemaphoreType.DMA((groups,)),
            pltpu.SemaphoreType.DMA,
        ],
        compiler_params=pltpu.CompilerParams(
            collective_id=0, has_side_effects=True, vmem_limit_bytes=VMEM_LIMIT
        ),
        name="exchange",
    )(features, idx.reshape(remote_rows, 1))

    activated, part, remote, owned = pl.pallas_call(
        layer_kernel,
        out_shape=(
            jax.ShapeDtypeStruct((rows_own, width), BF16),
            jax.ShapeDtypeStruct((width, width), F32),
            jax.ShapeDtypeStruct((remote_rows, width), BF16),
            jax.ShapeDtypeStruct((rows_own, width), F32),
        ),
        in_specs=[smem] * 4 + [any_] * 5,
        out_specs=(any_, vmem, any_, any_),
        scratch_shapes=[
            pltpu.VMEM((tiles + 1, edge, edge), BF16),
            pltpu.VMEM((rows_own + remote_rows, width), BF16),
            pltpu.VMEM((rows_own, width), BF16),
            pltpu.VMEM((width, width), BF16),
            pltpu.VMEM((rows_own, width), BF16),
            pltpu.VMEM((rows_own, width), BF16),
            pltpu.VMEM((rows_own, width), BF16),
            pltpu.VMEM((8, 128), BF16),
            pltpu.VMEM((edge, width), F32),
            pltpu.VMEM((remote_rows, width), BF16),
            pltpu.VMEM((rows_own, width), F32),
            pltpu.SemaphoreType.DMA((5,)),
        ],
        compiler_params=pltpu.CompilerParams(vmem_limit_bytes=VMEM_LIMIT),
        name="layer",
    )(order_f, start_f, order_b, start_b, features, arrived, tile_vals, weight, cotangent)

    chips = peers // 2
    grad, weight_grad = pl.pallas_call(
        functools.partial(return_kernel, groups, locals_, slots),
        out_shape=(
            jax.ShapeDtypeStruct((rows_own, width), BF16),
            jax.ShapeDtypeStruct((width, width), F32),
        ),
        in_specs=[any_, any_, vmem, vmem],
        out_specs=(vmem, vmem),
        scratch_shapes=[
            pltpu.VMEM((remote_rows, width), BF16),
            pltpu.VMEM((rows_own, width), F32),
            pltpu.VMEM((width // 2, width), F32),
            pltpu.VMEM((width // 2, width), F32),
            pltpu.VMEM((chips, 8, width * width // 2 // chips // 8), F32),
            pltpu.VMEM((8, width * width // 2 // chips // 8), F32),
            pltpu.SemaphoreType.DMA((groups,)),
            pltpu.SemaphoreType.DMA((groups,)),
            pltpu.SemaphoreType.DMA((2,)),
            pltpu.SemaphoreType.DMA((2,)),
            pltpu.SemaphoreType.DMA((2,)),
            pltpu.SemaphoreType.DMA,
            pltpu.SemaphoreType.DMA,
            pltpu.SemaphoreType.DMA,
            pltpu.SemaphoreType.DMA,
        ],
        compiler_params=pltpu.CompilerParams(
            collective_id=1, has_side_effects=True, vmem_limit_bytes=VMEM_LIMIT
        ),
        name="give_back",
    )(remote, owned, idx.reshape(1, remote_rows), part)
    return activated, grad, weight_grad


def solution(mesh):
    groups, locals_ = mesh.shape["group"], mesh.shape["local"]
    return jax.shard_map(
        functools.partial(per_device, groups, locals_),
        mesh=mesh,
        in_specs=(
            P(("group", "local"), None),
            P(),
            P(("group", "local"), None),
            P(("group", "local"), None, None),
            P(("group", "local")),
            P(("group", "local")),
            P(("group", "local"), None, None),
            P(("group", "local"), None),
        ),
        out_specs=(P(("group", "local"), None), P(("group", "local"), None), P()),
        check_vma=False,
    )
```

```python
import functools

import jax
import jax.numpy as jnp
from jax import lax
from jax.experimental import pallas as pl
from jax.experimental.pallas import tpu as pltpu
from jax.sharding import PartitionSpec as P

MESH = pl.DeviceIdType.MESH
F32 = jnp.float32
BF16 = jnp.bfloat16
VMEM_LIMIT = 60 * 1024 * 1024
EDGE = 128
SIDE = 4
SQUARE = 8
SQUARES = SIDE * SIDE
DEVICES = SQUARES * SQUARE
BATCHES = SQUARES // 2
PEERS = 2 * SQUARE


def span(at, size):
    return pl.ds(pl.multiple_of(at, size), size)


def wait_rows(ref, rows, sem):
    view = ref.at[pl.ds(0, rows)]
    pltpu.make_async_copy(view, view, sem).wait()


def network_kernel(
    cells, earlier,
    lists, live, feat_in, vals, weight_in, cot_in,
    activated, grad, wgrad,
    feat, tiles, rest, flipped, wbuf, cot, lst, rowtab, outgoing, arrived, acc, hid,
    returned, block, part, wsum, sib, chunks, gathered,
    load_sem, save_sem, send1, recv1, send2, recv2, sib_send, sib_recv, rs_send, rs_recv, ag_send, ag_recv,
):
    me = lax.axis_index("group") * (2 * SQUARE) + lax.axis_index("local")
    z, x = me // (SIDE * SQUARE), (me // SQUARE) % SIDE
    y, core = (me // 2) % SIDE, me % 2
    my_slot = y * 2 + core
    count = vals.shape[0]
    rows_own, width = feat.shape
    slots = lists.shape[1]
    row_blocks = rows_own // EDGE
    cols_all = row_blocks + DEVICES * slots // EDGE
    half_batch = SQUARE * slots
    batch = 2 * half_batch
    wide = batch // EDGE

    def device(square, slot):
        return (square // 2, (square % 2) * SQUARE + slot)

    def square_of(k, a, sign):
        dz, dx = k // SIDE + 2 * a, k % SIDE + 2 * a
        return ((z + SIDE + sign * dz) % SIDE) * SIDE + (x + 2 * SIDE + sign * dx) % SIDE

    loads = [
        pltpu.make_async_copy(feat_in, feat, load_sem.at[0]),
        pltpu.make_async_copy(vals, tiles.at[pl.ds(0, count)], load_sem.at[1]),
        pltpu.make_async_copy(cot_in, cot, load_sem.at[2]),
        pltpu.make_async_copy(weight_in, wbuf, load_sem.at[3]),
    ]
    for load in loads:
        load.start()

    barrier = pltpu.get_barrier_semaphore()

    @pl.loop(1, DEVICES)
    def _(k):
        peer = (me + k) % DEVICES
        pl.semaphore_signal(
            barrier, inc=1, device_id=device(peer // SQUARE, peer % SQUARE), device_id_type=MESH
        )

    lst[...] = jnp.full(lst.shape, -1, jnp.int32)
    limit = jnp.broadcast_to(live[...], (DEVICES, DEVICES)).T[:, :slots]
    lst[:, :slots] = jnp.where(
        lax.broadcasted_iota(jnp.int32, (DEVICES, slots), 1) < limit, lists[...], -1
    )

    def gather(k):
        picks = []
        for a in (0, 1):
            columns = lst[span(square_of(k, a, 1) * SQUARE, SQUARE), :].T
            picks += [columns[:slots, j : j + 1] for j in range(SQUARE)]
        ids = lax.broadcasted_iota(jnp.int32, (slots, rows_own), 1)
        onehot = jnp.concatenate([(pick == ids).astype(F32).astype(BF16) for pick in picks], axis=0)
        outgoing[span(k * batch, batch), :] = jnp.dot(
            onehot, feat[...], preferred_element_type=F32
        ).astype(BF16)

    def send(k, i, landing, send_sem, recv_sem):
        a, dy, dc = i % 2, (2 + i // 2) % SIDE, i // SQUARE
        slot = ((y + dy) % SIDE) * 2 + (core + dc) % 2
        base = k * batch + a * half_batch
        pltpu.make_async_remote_copy(
            src_ref=outgoing.at[span(base + slot * slots, slots)],
            dst_ref=landing.at[span(base + my_slot * slots, slots)],
            send_sem=send_sem.at[k],
            recv_sem=recv_sem.at[k],
            device_id=device(square_of(k, a, 1), slot),
            device_id_type=MESH,
        ).start()

    def send_first(landing, send_sem, recv_sem):
        for i in range(PEERS):
            if i != 4:
                send(0, i, landing, send_sem, recv_sem)
        mine = span(my_slot * slots, slots)
        landing[mine, :] = outgoing[mine, :]

    def send_batch(k, landing, send_sem, recv_sem):
        @pl.loop(0, PEERS)
        def _(i):
            send(k, i, landing, send_sem, recv_sem)

    loads[0].wait()
    gather(0)
    pl.semaphore_wait(barrier, DEVICES - 1)
    send_first(arrived, send1, recv1)

    @pl.loop(1, BATCHES)
    def _(k):
        gather(k)
        send_batch(k, arrived, send1, recv1)

    for empty in (tiles, rest, flipped):
        empty[count] = jnp.zeros((EDGE, EDGE), BF16)
    loads[1].wait()

    @pl.loop(0, count)
    def _(t):
        before = earlier[t]
        exact = tiles[t].astype(F32) + (tiles[before].astype(F32) + rest[before].astype(F32))
        merged = exact.astype(BF16)
        rest[t] = (exact - merged.astype(F32)).astype(BF16)
        tiles[t] = merged
        flipped[t] = merged.T

    lane = lax.broadcasted_iota(jnp.int32, (SQUARES, EDGE), 1) // slots
    per = EDGE // slots
    for h in range(SQUARE // per):
        line = jnp.full((SQUARES, EDGE), -1, jnp.int32)
        for j in range(per):
            row = lst[pl.ds(h * per + j, SQUARES, stride=SQUARE), :]
            line = jnp.where(lane == j, pltpu.roll(row, j * slots, 1) if j else row, line)
        rowtab[:, h * EDGE : (h + 1) * EDGE] = line

    def remote_cols(k, sign):
        per_square = half_batch // EDGE
        first = [row_blocks + square_of(k, a, sign) * per_square for a in (0, 1)]
        return [f + n for f in first for n in range(per_square)]

    def forward(cols, source, fresh):
        @pl.loop(0, row_blocks // wide)
        def _(m):
            left = jnp.concatenate(
                [
                    jnp.concatenate([tiles[cells[(m * wide + r) * cols_all + c]] for c in cols], axis=1)
                    for r in range(wide)
                ],
                axis=0,
            )
            product = jnp.dot(left, source, preferred_element_type=F32)
            at = span(m * batch, batch)
            if fresh:
                acc[at, :] = product
            else:
                acc[at, :] += product

    def own_cols(n):
        return [n * wide + j for j in range(wide)]

    forward(own_cols(0), feat[span(0, batch), :], True)

    @pl.loop(1, row_blocks // wide)
    def _(n):
        forward(own_cols(n), feat[span(n * batch, batch), :], False)

    def take_batch(k):
        forward(remote_cols(k, -1), arrived[span(k * batch, batch), :], False)

    wait_rows(arrived, batch - slots, recv1.at[0])
    take_batch(0)

    @pl.loop(1, BATCHES)
    def _(k):
        wait_rows(arrived, batch, recv1.at[k])
        take_batch(k)

    loads[2].wait()
    loads[3].wait()

    slope, hgrad = arrived.at[pl.ds(0, rows_own)], arrived.at[pl.ds(rows_own, rows_own)]

    @pl.loop(0, rows_own // batch)
    def _(b):
        at = span(b * batch, batch)
        h = acc[at, :].astype(BF16)
        hid[at, :] = h
        pre = jnp.dot(h, wbuf[...], preferred_element_type=F32)
        gate = jax.nn.sigmoid(pre)
        s = (cot[at, :].astype(F32) * gate * (1.0 + pre * (1.0 - gate))).astype(BF16)
        cot[at, :] = (pre * gate).astype(BF16)
        slope[at, :] = s
        hgrad[at, :] = lax.dot_general(
            s, wbuf[...], (((1,), (1,)), ((), ())), preferred_element_type=F32
        ).astype(BF16)

    save_act = pltpu.make_async_copy(cot, activated, save_sem)
    save_act.start()

    def spread(cols):
        block[...] = jnp.zeros_like(block)

        @pl.loop(0, row_blocks // wide)
        def _(m):
            left = jnp.concatenate(
                [
                    jnp.concatenate([flipped[cells[(m * wide + r) * cols_all + c]] for r in range(wide)], axis=1)
                    for c in cols
                ],
                axis=0,
            )
            block[...] += jnp.dot(left, hgrad[span(m * batch, batch), :], preferred_element_type=F32)

    def give(k):
        spread(remote_cols(k, 1))
        outgoing[span(k * batch, batch), :] = block[...].astype(BF16)

    wait_rows(outgoing, batch - slots, send1.at[0])
    give(0)
    send_first(returned, send2, recv2)

    part[...] = jnp.zeros_like(part)

    @pl.loop(0, rows_own // batch)
    def _(b):
        at = span(b * batch, batch)
        part[...] += lax.dot_general(
            hid[at, :], slope[at, :], (((0,), (0,)), ((), ())), preferred_element_type=F32
        )

    half = width // 2
    mine, other = pl.multiple_of(core * half, half), pl.multiple_of((1 - core) * half, half)
    chips = DEVICES // 2
    chip = me // 2
    square = me // SQUARE
    edge_r, edge_c = chunks.shape[1:]
    across = width // edge_c
    sibling = device(square, y * 2 + 1 - core)
    swap = pltpu.make_async_remote_copy(
        src_ref=part.at[pl.ds(other, half)],
        dst_ref=sib,
        send_sem=sib_send.at[0],
        recv_sem=sib_recv.at[0],
        device_id=sibling,
        device_id_type=MESH,
    )
    swap.start()

    wait_rows(outgoing, batch, send1.at[1])
    give(1)
    send_batch(1, returned, send2, recv2)
    swap.wait()
    wsum[...] = part[pl.ds(mine, half), :] + sib[...]

    def spot(q):
        return q // across * edge_r, q % across * edge_c

    def mate(q):
        return device(q // SIDE, q % SIDE * 2 + core)

    @pl.loop(1, chips)
    def _(k):
        q = (chip + k) % chips
        r0, c0 = spot(q)
        pltpu.make_async_remote_copy(
            src_ref=wsum.at[span(r0, edge_r), span(c0, edge_c)],
            dst_ref=chunks.at[chip],
            send_sem=rs_send,
            recv_sem=rs_recv,
            device_id=mate(q),
            device_id_type=MESH,
        ).start()

    r0, c0 = spot(chip)
    chunks[chip] = wsum[span(r0, edge_r), span(c0, edge_c)]

    @pl.loop(2, BATCHES)
    def _(k):
        wait_rows(outgoing, batch, send1.at[k])
        give(k)
        send_batch(k, returned, send2, recv2)

    wait_rows(chunks, chips - 1, rs_send)
    wait_rows(chunks, chips - 1, rs_recv)
    gathered[...] = jnp.sum(chunks[...], axis=0)
    there = (span(mine + r0, edge_r), span(c0, edge_c))
    wgrad[there[0], there[1]] = gathered[...]

    @pl.loop(1, chips)
    def _(k):
        pltpu.make_async_remote_copy(
            src_ref=gathered,
            dst_ref=wgrad.at[there[0], there[1]],
            send_sem=ag_send,
            recv_sem=ag_recv,
            device_id=mate((chip + k) % chips),
            device_id_type=MESH,
        ).start()

    @pl.loop(0, row_blocks // wide)
    def _(n):
        spread(own_cols(n))
        acc[span(n * batch, batch), :] = block[...]

    def add_batch(k):
        picks = jnp.concatenate([rowtab[pl.ds(square_of(k, a, -1), 1), :] for a in (0, 1)], axis=1)
        rows = returned[span(k * batch, batch), :]

        @pl.loop(0, rows_own // 1024)
        def _(b):
            ids = lax.broadcasted_iota(jnp.int32, (1024, batch), 0) + b * 1024
            onehot = (ids == picks).astype(F32).astype(BF16)
            acc[span(b * 1024, 1024), :] += jnp.dot(onehot, rows, preferred_element_type=F32)

    wait_rows(returned, batch - slots, recv2.at[0])
    add_batch(0)

    @pl.loop(1, BATCHES)
    def _(k):
        wait_rows(returned, batch, recv2.at[k])
        add_batch(k)

    wait_rows(chunks, chips - 1, ag_send)
    wait_rows(chunks, chips - 1, ag_recv)
    back = pltpu.make_async_remote_copy(
        src_ref=wgrad.at[pl.ds(mine, half)],
        dst_ref=wgrad.at[pl.ds(mine, half)],
        send_sem=sib_send.at[1],
        recv_sem=sib_recv.at[1],
        device_id=sibling,
        device_id_type=MESH,
    )
    back.start()
    grad[...] = acc[...].astype(BF16)
    wait_rows(returned, batch - slots, send2.at[0])

    @pl.loop(1, BATCHES)
    def _(k):
        wait_rows(returned, batch, send2.at[k])

    save_act.wait()
    back.wait()


def per_device(features, weight, cotangent, tile_vals, tile_rows, tile_cols, send_rows, counts):
    rows_own, width = features.shape
    count = tile_vals.shape[0]
    slots = send_rows.shape[2]
    row_blocks = rows_own // EDGE
    remote_rows = DEVICES * slots
    cols_all = row_blocks + remote_rows // EDGE
    batch = 2 * SQUARE * slots

    ids = jnp.arange(count, dtype=jnp.int32)
    cell = tile_rows * cols_all + tile_cols
    same = (cell[None, :] == cell[:, None]) & (ids[None, :] < ids[:, None])
    earlier = jnp.max(jnp.where(same, ids[None, :], -1), axis=1)
    earlier = jnp.where(earlier < 0, count, earlier)
    there = cell[None, :] == jnp.arange(row_blocks * cols_all, dtype=jnp.int32)[:, None]
    cells = jnp.max(jnp.where(there, ids[None, :], -1), axis=1)
    cells = jnp.where(cells < 0, count, cells)

    any_ = pl.BlockSpec(memory_space=pl.ANY)
    vmem = pl.BlockSpec(memory_space=pltpu.VMEM)
    smem = pl.BlockSpec(memory_space=pltpu.SMEM)
    chips = DEVICES // 2
    edge_c = width * width // 2 // chips // 8
    dma = pltpu.SemaphoreType.DMA
    rows16 = pltpu.VMEM((rows_own, width), BF16)
    far16 = pltpu.VMEM((remote_rows, width), BF16)
    activated, grad, weight_grad = pl.pallas_call(
        network_kernel,
        out_shape=(
            jax.ShapeDtypeStruct((rows_own, width), BF16),
            jax.ShapeDtypeStruct((rows_own, width), BF16),
            jax.ShapeDtypeStruct((width, width), F32),
        ),
        in_specs=[smem, smem, vmem, vmem] + [any_] * 4,
        out_specs=(any_, vmem, vmem),
        scratch_shapes=[
            rows16,
            pltpu.VMEM((count + 1, EDGE, EDGE), BF16),
            pltpu.VMEM((count + 1, EDGE, EDGE), BF16),
            pltpu.VMEM((count + 1, EDGE, EDGE), BF16),
            pltpu.VMEM((width, width), BF16),
            rows16,
            pltpu.VMEM((DEVICES, EDGE), jnp.int32),
            pltpu.VMEM((SQUARES, SQUARE * slots), jnp.int32),
            far16,
            far16,
            pltpu.VMEM((rows_own, width), F32),
            rows16,
            far16,
            pltpu.VMEM((batch, width), F32),
            pltpu.VMEM((width, width), F32),
            pltpu.VMEM((width // 2, width), F32),
            pltpu.VMEM((width // 2, width), F32),
            pltpu.VMEM((chips, 8, edge_c), F32),
            pltpu.VMEM((8, edge_c), F32),
            dma((4,)),
            dma,
            dma((BATCHES,)),
            dma((BATCHES,)),
            dma((BATCHES,)),
            dma((BATCHES,)),
            dma((2,)),
            dma((2,)),
            dma,
            dma,
            dma,
            dma,
        ],
        compiler_params=pltpu.CompilerParams(
            collective_id=0, has_side_effects=True, vmem_limit_bytes=VMEM_LIMIT
        ),
        name="network",
    )(cells, earlier, send_rows[0], counts, features, tile_vals, weight, cotangent)
    return activated, grad, weight_grad


def solution(mesh):
    rows = P(("group", "local"), None)
    tiles = P(("group", "local"), None, None)
    flat = P(("group", "local"))
    return jax.shard_map(
        per_device,
        mesh=mesh,
        in_specs=(rows, P(), rows, tiles, flat, flat, tiles, rows),
        out_specs=(rows, rows, P()),
        check_vma=False,
    )
```

```python
import functools

import jax
import jax.numpy as jnp
from jax import lax
from jax.experimental import pallas as pl
from jax.experimental.pallas import tpu as pltpu
from jax.sharding import PartitionSpec as P

MESH = pl.DeviceIdType.MESH
F32 = jnp.float32
BF16 = jnp.bfloat16
VMEM_LIMIT = 60 * 1024 * 1024
EDGE = 128
SIDE = 4
SQUARE = 8
SQUARES = SIDE * SIDE
DEVICES = SQUARES * SQUARE
BATCHES = SQUARES // 2
PARTS = 4


def div(a, b):
    return a // b if isinstance(a, int) else lax.div(a, b)


def rem(a, b):
    return a % b if isinstance(a, int) else lax.rem(a, b)


def span(at, size):
    return pl.ds(pl.multiple_of(at, size), size)


def wait_rows(ref, rows, sem):
    view = ref.at[pl.ds(0, rows)]
    pltpu.make_async_copy(view, view, sem).wait()


def network_kernel(
    lists, live, tile_rows, tile_cols, feat_in, vals, weight_in, cot_in,
    activated, grad, wgrad,
    plan_v, plan, feat, tiles, rest, flipped, wbuf, cot, lst, rowtab, outgoing, arrived, acc, hid, slope, hgrad,
    returned, part, wsum, sib, chunks, gathered, wall,
    load_sem, save_sem, send1, recv1, send2, recv2, sib_send, sib_recv, rs_send, rs_recv, ag_send, ag_recv,
):
    me = lax.axis_index("group") * (2 * SQUARE) + lax.axis_index("local")
    z, x = div(me, SIDE * SQUARE), rem(div(me, SQUARE), SIDE)
    y, core = rem(div(me, 2), SIDE), rem(me, 2)
    my_slot = y * 2 + core
    count = vals.shape[0]
    rows_own, width = feat.shape
    slots = lists.shape[0]
    row_blocks = rows_own // EDGE
    cols_all = row_blocks + DEVICES * slots // EDGE
    half_batch = SQUARE * slots
    batch = 2 * half_batch
    wide = batch // EDGE

    def device(square, slot):
        return (div(square, 2), rem(square, 2) * SQUARE + slot)

    def square_of(k, a, sign):
        dz, dx = div(k, SIDE) + 2 * a, rem(k, SIDE) + 2 * a
        return rem(z + SIDE + sign * dz, SIDE) * SIDE + rem(x + 2 * SIDE + sign * dx, SIDE)

    loads = [
        pltpu.make_async_copy(feat_in, feat, load_sem.at[0]),
        pltpu.make_async_copy(vals, tiles.at[pl.ds(0, count)], load_sem.at[1]),
        pltpu.make_async_copy(cot_in, cot, load_sem.at[2]),
        pltpu.make_async_copy(weight_in, wbuf, load_sem.at[3]),
    ]
    for load in loads:
        load.start()

    barrier = pltpu.get_barrier_semaphore()

    def greet(square, slot):
        pl.semaphore_signal(barrier, inc=1, device_id=device(square, slot), device_id_type=MESH)

    my_square = div(me, SQUARE)
    for j in range(1, SQUARE):
        greet(my_square, rem(my_slot + j, SQUARE))

    @pl.loop(1, SQUARES)
    def _(k):
        square = rem(my_square + k, SQUARES)
        for j in range(SQUARE):
            greet(square, j)

    rank = lax.broadcasted_iota(jnp.int32, (slots, DEVICES), 0)
    masked = jnp.where(rank < live[...], lists[...], -1)
    lst[...] = jnp.concatenate([masked, jnp.full((EDGE - slots, DEVICES), -1, jnp.int32)], axis=0).T

    def gather(k):
        picks = []
        for a in (0, 1):
            columns = lst[span(square_of(k, a, 1) * SQUARE, SQUARE), :].T
            picks += [columns[:slots, j : j + 1] for j in range(SQUARE)]
        ids = lax.broadcasted_iota(jnp.int32, (slots, rows_own), 1)
        onehot = jnp.concatenate([(pick == ids).astype(F32).astype(BF16) for pick in picks], axis=0)
        outgoing[span(k * batch, batch), :] = jnp.dot(
            onehot, feat[...], preferred_element_type=F32
        ).astype(BF16)

    slot_at = {
        (dy, dc): rem(y + dy, SIDE) * 2 + rem(core + dc, 2) for dy in range(SIDE) for dc in range(2)
    }

    def send_batch(k, landing, send_sem, recv_sem, with_self=False):
        squares = [square_of(k, a, 1) for a in (0, 1)]
        bases = [pl.multiple_of(k * batch + a * half_batch, half_batch) for a in (0, 1)]
        for dc in (0, 1):
            for dy in (2, 3, 0, 1):
                for a in (0, 1):
                    if with_self and (a, dy, dc) == (0, 0, 0):
                        continue
                    slot = slot_at[dy, dc]
                    pltpu.make_async_remote_copy(
                        src_ref=outgoing.at[span(bases[a] + slot * slots, slots)],
                        dst_ref=landing.at[span(bases[a] + my_slot * slots, slots)],
                        send_sem=send_sem.at[k],
                        recv_sem=recv_sem.at[k],
                        device_id=device(squares[a], slot),
                        device_id_type=MESH,
                    ).start()

    def send_first(landing, send_sem, recv_sem):
        send_batch(0, landing, send_sem, recv_sem, True)
        mine = span(my_slot * slots, slots)
        landing[mine, :] = outgoing[mine, :]

    loads[0].wait()
    gather(0)
    pl.semaphore_wait(barrier, DEVICES - 1)
    send_first(arrived, send1, recv1)

    @pl.loop(1, BATCHES)
    def _(k):
        gather(k)
        send_batch(k, arrived, send1, recv1)

    keys = tile_rows[...] * cols_all + tile_cols[...]
    column = jnp.broadcast_to(keys, (EDGE, count)).T
    tile_ids = lax.broadcasted_iota(jnp.int32, (count, EDGE), 0)
    lanes = lax.broadcasted_iota(jnp.int32, (1, EDGE), 1)

    def last_of(hit):
        found = jnp.max(jnp.where(hit, tile_ids, -1), axis=0, keepdims=True)
        return jnp.where(found < 0, count, found)

    for r in range(row_blocks):
        plan_v[r : r + 1, :] = last_of((column == r * cols_all + lanes) & (lanes < cols_all))
    for h in range(count // EDGE):
        own = keys[:, h * EDGE : (h + 1) * EDGE]
        plan_v[row_blocks + h : row_blocks + h + 1, :] = last_of(
            (column == own) & (tile_ids < lanes + h * EDGE)
        )
    save_plan = pltpu.make_async_copy(plan_v, plan, save_sem)
    save_plan.start()
    save_plan.wait()

    for empty in (tiles, rest, flipped):
        empty[count] = jnp.zeros((EDGE, EDGE), BF16)
    loads[1].wait()

    unroll = 4
    for h in range(count // EDGE):

        @pl.loop(0, EDGE // unroll)
        def _(i):
            for u in range(unroll):
                t = h * EDGE + i * unroll + u
                before = plan[row_blocks + h, i * unroll + u]
                exact = tiles[t].astype(F32) + (tiles[before].astype(F32) + rest[before].astype(F32))
                merged = exact.astype(BF16)
                rest[t] = (exact - merged.astype(F32)).astype(BF16)
                tiles[t] = merged

    @pl.loop(0, count // 8)
    def _(i):
        for u in range(8):
            flipped[i * 8 + u] = tiles[i * 8 + u].T

    lane = lax.broadcasted_iota(jnp.int32, (SQUARES, EDGE), 1) // slots
    per = EDGE // slots
    for h in range(SQUARE // per):
        line = jnp.full((SQUARES, EDGE), -1, jnp.int32)
        for j in range(per):
            row = lst[pl.ds(h * per + j, SQUARES, stride=SQUARE), :]
            line = jnp.where(lane == j, pltpu.roll(row, j * slots, 1) if j else row, line)
        rowtab[:, h * EDGE : (h + 1) * EDGE] = line

    def remote_cols(k, sign):
        per_square = half_batch // EDGE
        first = [row_blocks + square_of(k, a, sign) * per_square for a in (0, 1)]
        return [f + n for f in first for n in range(per_square)]

    def left_of(cols, m):
        bands = [
            jnp.concatenate([tiles[plan[m * wide + r, c]] for c in cols], axis=1) for r in range(wide)
        ]
        return jnp.concatenate(bands, axis=0)

    @pl.loop(0, row_blocks // wide)
    def _(m):
        acc[span(m * batch, batch), :] = jnp.dot(
            left_of(range(row_blocks), m), feat[...], preferred_element_type=F32
        )

    def take(cols, source):
        @pl.loop(0, row_blocks // wide)
        def _(m):
            acc[span(m * batch, batch), :] += jnp.dot(left_of(cols, m), source, preferred_element_type=F32)

    wait_rows(arrived, batch - slots, recv1.at[0])
    take(remote_cols(0, -1), arrived[span(0, batch), :])

    @pl.loop(0, (BATCHES - 2) // 2)
    def _(i):
        k = 1 + 2 * i
        for n in (0, 1):
            wait_rows(arrived, batch, recv1.at[k + n])
        take(remote_cols(k, -1) + remote_cols(k + 1, -1), arrived[pl.ds(pl.multiple_of(k * batch, batch), 2 * batch), :])

    loads[2].wait()
    loads[3].wait()
    last = BATCHES - 1
    wait_rows(arrived, batch, recv1.at[last])
    cols = remote_cols(last, -1)
    source = arrived[span(last * batch, batch), :]
    for b in range(rows_own // batch):
        at = pl.ds(b * batch, batch)
        h = (acc[at, :] + jnp.dot(left_of(cols, b), source, preferred_element_type=F32)).astype(BF16)
        hid[at, :] = h
        pre = jnp.dot(h, wbuf[...], preferred_element_type=F32)
        gate = jax.nn.sigmoid(pre)
        s = (cot[at, :].astype(F32) * gate * (1.0 + pre * (1.0 - gate))).astype(BF16)
        cot[at, :] = (pre * gate).astype(BF16)
        slope[at, :] = s
        hgrad[at, :] = lax.dot_general(
            s, wbuf[...], (((1,), (1,)), ((), ())), preferred_element_type=F32
        ).astype(BF16)

    save_act = pltpu.make_async_copy(cot, activated, save_sem)
    save_act.start()

    def spread(cols):
        bands = [
            jnp.concatenate([flipped[plan[r, c]] for r in range(row_blocks)], axis=1) for c in cols
        ]
        return jnp.dot(jnp.concatenate(bands, axis=0), hgrad[...], preferred_element_type=F32)

    def give(k):
        outgoing[span(k * batch, batch), :] = spread(remote_cols(k, 1)).astype(BF16)

    wait_rows(outgoing, batch - slots, send1.at[0])
    give(0)
    send_first(returned, send2, recv2)

    part[...] = jnp.zeros_like(part)

    @pl.loop(0, rows_own // batch)
    def _(b):
        at = span(b * batch, batch)
        part[...] += lax.dot_general(
            hid[at, :], slope[at, :], (((0,), (0,)), ((), ())), preferred_element_type=F32
        )

    half = width // 2
    mine, other = pl.multiple_of(core * half, half), pl.multiple_of((1 - core) * half, half)
    chips = DEVICES // 2
    chip = div(me, 2)
    square = div(me, SQUARE)
    edge_r, edge_c = chunks.shape[1:]
    across = width // edge_c
    sibling = device(square, y * 2 + 1 - core)
    swap = pltpu.make_async_remote_copy(
        src_ref=part.at[pl.ds(other, half)],
        dst_ref=sib,
        send_sem=sib_send.at[0],
        recv_sem=sib_recv.at[0],
        device_id=sibling,
        device_id_type=MESH,
    )
    swap.start()

    wait_rows(outgoing, batch, send1.at[1])
    give(1)
    send_batch(1, returned, send2, recv2)
    swap.wait()
    wsum[...] = (part[pl.ds(mine, half), :] + sib[...]).astype(BF16)

    def spot(q):
        return div(q, across) * edge_r, rem(q, across) * edge_c

    def mate(q):
        return device(div(q, SIDE), rem(q, SIDE) * 2 + core)

    @pl.loop(1, chips)
    def _(k):
        q = rem(chip + k, chips)
        r0, c0 = spot(q)
        pltpu.make_async_remote_copy(
            src_ref=wsum.at[span(r0, edge_r), span(c0, edge_c)],
            dst_ref=chunks.at[chip],
            send_sem=rs_send,
            recv_sem=rs_recv,
            device_id=mate(q),
            device_id_type=MESH,
        ).start()

    r0, c0 = spot(chip)
    chunks[chip] = wsum[span(r0, edge_r), span(c0, edge_c)]

    def give_batch(k):
        wait_rows(outgoing, batch, send1.at[k])
        give(k)
        send_batch(k, returned, send2, recv2)

    @pl.loop(2, BATCHES // 2)
    def _(k):
        give_batch(k)

    @pl.loop(0, row_blocks // wide)
    def _(n):
        acc[span(n * batch, batch), :] = spread([n * wide + j for j in range(wide)])

    wait_rows(chunks, chips - 1, rs_send)
    wait_rows(chunks, chips - 1, rs_recv)
    gathered[...] = jnp.sum(chunks[...].astype(F32), axis=0).astype(BF16)
    there = (span(mine + r0, edge_r), span(c0, edge_c))
    wall[there[0], there[1]] = gathered[...]

    @pl.loop(1, chips)
    def _(k):
        pltpu.make_async_remote_copy(
            src_ref=gathered,
            dst_ref=wall.at[there[0], there[1]],
            send_sem=ag_send,
            recv_sem=ag_recv,
            device_id=mate(rem(chip + k, chips)),
            device_id_type=MESH,
        ).start()

    @pl.loop(BATCHES // 2, BATCHES)
    def _(k):
        give_batch(k)

    tall = 1024

    def picks_of(k):
        return jnp.concatenate([rowtab[pl.ds(square_of(k, a, -1), 1), :] for a in (0, 1)], axis=1)

    def hits(picks, rows, b):
        ids = lax.broadcasted_iota(jnp.int32, (tall, batch), 0) + b * tall
        onehot = (ids == picks).astype(F32).astype(BF16)
        return jnp.dot(onehot, rows, preferred_element_type=F32)

    def add_batch(k):
        picks, rows = picks_of(k), returned[span(k * batch, batch), :]

        @pl.loop(0, rows_own // tall)
        def _(b):
            acc[span(b * tall, tall), :] += hits(picks, rows, b)

    def take_back(k):
        wait_rows(returned, batch, recv2.at[k])
        add_batch(k)

    wait_rows(returned, batch - slots, recv2.at[0])
    add_batch(0)

    @pl.loop(1, BATCHES // 2 + 1)
    def _(k):
        take_back(k)

    wait_rows(chunks, chips - 1, ag_send)
    wait_rows(chunks, chips - 1, ag_recv)
    back = pltpu.make_async_remote_copy(
        src_ref=wall.at[pl.ds(mine, half)],
        dst_ref=wall.at[pl.ds(mine, half)],
        send_sem=sib_send.at[1],
        recv_sem=sib_recv.at[1],
        device_id=sibling,
        device_id_type=MESH,
    )
    back.start()

    @pl.loop(BATCHES // 2 + 1, last)
    def _(k):
        take_back(k)

    back.wait()
    save_wall = pltpu.make_async_copy(wall, wgrad, save_sem)
    save_act.wait()
    save_wall.start()
    wait_rows(returned, batch, recv2.at[last])
    picks, rows = picks_of(last), returned[span(last * batch, batch), :]
    saves = []
    for b in range(rows_own // tall):
        at = pl.ds(b * tall, tall)
        hid[at, :] = (acc[at, :] + hits(picks, rows, b)).astype(BF16)
        saves.append(pltpu.make_async_copy(hid.at[at], grad.at[at], load_sem.at[b]))
        saves[-1].start()
    wait_rows(returned, batch - slots, send2.at[0])

    @pl.loop(1, BATCHES)
    def _(k):
        wait_rows(returned, batch, send2.at[k])

    for save in saves:
        save.wait()
    save_wall.wait()


def deliver_kernel(act_in, grad_in, wgrad_in, act_out, grad_out, wgrad_out, act, grad, load_sem, save_sem):
    loads, saves = [], []
    for n, (src, via, dst) in enumerate(((act_in, act, act_out), (grad_in, grad, grad_out))):
        rows = src.shape[0] // PARTS
        for p in range(PARTS):
            at = pl.ds(p * rows, rows)
            loads.append(pltpu.make_async_copy(src.at[at], via.at[at], load_sem.at[n, p]))
            saves.append(pltpu.make_async_copy(via.at[at], dst.at[at], save_sem.at[n, p]))
    for load in loads:
        load.start()
    wgrad_out[...] = wgrad_in[...].astype(F32)
    for load, save in zip(loads, saves):
        load.wait()
        save.start()
    for save in saves:
        save.wait()


def per_device(features, weight, cotangent, tile_vals, tile_rows, tile_cols, send_rows, counts):
    rows_own, width = features.shape
    count = tile_vals.shape[0]
    slots = send_rows.shape[2]
    row_blocks = rows_own // EDGE
    remote_rows = DEVICES * slots
    cols_all = row_blocks + remote_rows // EDGE
    batch = 2 * SQUARE * slots

    any_ = pl.BlockSpec(memory_space=pl.ANY)
    vmem = pl.BlockSpec(memory_space=pltpu.VMEM)
    chips = DEVICES // 2
    edge_r = width * width // 2 // chips // EDGE
    dma = pltpu.SemaphoreType.DMA
    rows16 = pltpu.VMEM((rows_own, width), BF16)
    far16 = pltpu.VMEM((remote_rows, width), BF16)
    activated, grad, weight_grad = pl.pallas_call(
        network_kernel,
        out_shape=(
            jax.ShapeDtypeStruct((rows_own, width), BF16),
            jax.ShapeDtypeStruct((rows_own, width), BF16),
            jax.ShapeDtypeStruct((width, width), BF16),
        ),
        in_specs=[vmem] * 4 + [any_] * 4,
        out_specs=(any_,) * 3,
        scratch_shapes=[
            pltpu.VMEM((24, EDGE), jnp.int32),
            pltpu.SMEM((24, EDGE), jnp.int32),
            rows16,
            pltpu.VMEM((count + 1, EDGE, EDGE), BF16),
            pltpu.VMEM((count + 1, EDGE, EDGE), BF16),
            pltpu.VMEM((count + 1, EDGE, EDGE), BF16),
            pltpu.VMEM((width, width), BF16),
            rows16,
            pltpu.VMEM((DEVICES, EDGE), jnp.int32),
            pltpu.VMEM((SQUARES, SQUARE * slots), jnp.int32),
            far16,
            far16,
            pltpu.VMEM((rows_own, width), F32),
            rows16,
            rows16,
            rows16,
            far16,
            pltpu.VMEM((width, width), F32),
            pltpu.VMEM((width // 2, width), BF16),
            pltpu.VMEM((width // 2, width), F32),
            pltpu.VMEM((chips, edge_r, EDGE), BF16),
            pltpu.VMEM((edge_r, EDGE), BF16),
            pltpu.VMEM((width, width), BF16),
            dma((4,)),
            dma,
            dma((BATCHES,)),
            dma((BATCHES,)),
            dma((BATCHES,)),
            dma((BATCHES,)),
            dma((2,)),
            dma((2,)),
            dma,
            dma,
            dma,
            dma,
        ],
        compiler_params=pltpu.CompilerParams(
            collective_id=0, has_side_effects=True, vmem_limit_bytes=VMEM_LIMIT
        ),
        name="network",
    )(send_rows[0].T, counts, tile_rows.reshape(1, count), tile_cols.reshape(1, count), features, tile_vals, weight, cotangent)
    return pl.pallas_call(
        deliver_kernel,
        out_shape=(
            jax.ShapeDtypeStruct((rows_own, width), BF16),
            jax.ShapeDtypeStruct((rows_own, width), BF16),
            jax.ShapeDtypeStruct((width, width), F32),
        ),
        in_specs=[any_, any_, vmem],
        out_specs=(any_, any_, vmem),
        scratch_shapes=[rows16, rows16, dma((2, PARTS)), dma((2, PARTS))],
        compiler_params=pltpu.CompilerParams(vmem_limit_bytes=VMEM_LIMIT),
        name="deliver",
    )(activated, grad, weight_grad)


def solution(mesh):
    rows = P(("group", "local"), None)
    tiles = P(("group", "local"), None, None)
    flat = P(("group", "local"))
    return jax.shard_map(
        per_device,
        mesh=mesh,
        in_specs=(rows, P(), rows, tiles, flat, flat, tiles, rows),
        out_specs=(rows, rows, P()),
        check_vma=False,
    )
```

```python
import functools

import jax
import jax.numpy as jnp
from jax import lax
from jax.experimental import pallas as pl
from jax.experimental.pallas import tpu as pltpu
from jax.sharding import PartitionSpec as P

MESH = pl.DeviceIdType.MESH
F32 = jnp.float32
BF16 = jnp.bfloat16
VMEM_LIMIT = 60 * 1024 * 1024
EDGE = 128
SIDE = 4
SQUARE = 8
SQUARES = SIDE * SIDE
DEVICES = SQUARES * SQUARE
BATCHES = SQUARES // 2
PARTS = 4


def div(a, b):
    return a // b if isinstance(a, int) else lax.div(a, b)


def rem(a, b):
    return a % b if isinstance(a, int) else lax.rem(a, b)


def span(at, size):
    return pl.ds(pl.multiple_of(at, size), size)


def wait_rows(ref, rows, sem):
    view = ref.at[pl.ds(0, rows)]
    pltpu.make_async_copy(view, view, sem).wait()


def network_kernel(
    lists, live, tile_rows, tile_cols, feat_in, vals, weight_in, cot_in,
    activated, grad, wgrad,
    plan_v, plan, feat, tiles, rest, flipped, wbuf, cot, lst, rowtab, outgoing, arrived, acc, hid, slope, hgrad,
    returned, part, wsum, sib, chunks, gathered, wall,
    load_sem, save_sem, send1, recv1, send2, recv2, sib_send, sib_recv, rs_send, rs_recv, ag_send, ag_recv,
):
    me = lax.axis_index("group") * (2 * SQUARE) + lax.axis_index("local")
    z, x = div(me, SIDE * SQUARE), rem(div(me, SQUARE), SIDE)
    y, core = rem(div(me, 2), SIDE), rem(me, 2)
    my_slot = y * 2 + core
    count = vals.shape[0]
    rows_own, width = feat.shape
    slots = lists.shape[0]
    row_blocks = rows_own // EDGE
    cols_all = row_blocks + DEVICES * slots // EDGE
    half_batch = SQUARE * slots
    batch = 2 * half_batch
    wide = batch // EDGE

    def device(square, slot):
        return (div(square, 2), rem(square, 2) * SQUARE + slot)

    def square_of(k, a, sign):
        dz, dx = div(k, SIDE) + 2 * a, rem(k, SIDE) + 2 * a
        return rem(z + SIDE + sign * dz, SIDE) * SIDE + rem(x + 2 * SIDE + sign * dx, SIDE)

    loads = [
        pltpu.make_async_copy(feat_in, feat, load_sem.at[0]),
        pltpu.make_async_copy(vals, tiles.at[pl.ds(0, count)], load_sem.at[1]),
        pltpu.make_async_copy(cot_in, cot, load_sem.at[2]),
        pltpu.make_async_copy(weight_in, wbuf, load_sem.at[3]),
    ]
    for load in loads:
        load.start()

    barrier = pltpu.get_barrier_semaphore()

    def greet(square, slot):
        pl.semaphore_signal(barrier, inc=1, device_id=device(square, slot), device_id_type=MESH)

    my_square = div(me, SQUARE)
    for j in range(1, SQUARE):
        greet(my_square, rem(my_slot + j, SQUARE))

    @pl.loop(1, SQUARES)
    def _(k):
        square = rem(my_square + k, SQUARES)
        for j in range(SQUARE):
            greet(square, j)

    rank = lax.broadcasted_iota(jnp.int32, (slots, DEVICES), 0)
    masked = jnp.where(rank < live[...], lists[...], -1)
    lst[...] = jnp.concatenate([masked, jnp.full((EDGE - slots, DEVICES), -1, jnp.int32)], axis=0).T

    def gather(k):
        picks = []
        for a in (0, 1):
            columns = lst[span(square_of(k, a, 1) * SQUARE, SQUARE), :].T
            picks += [columns[:slots, j : j + 1] for j in range(SQUARE)]
        ids = lax.broadcasted_iota(jnp.int32, (slots, rows_own), 1)
        onehot = jnp.concatenate([(pick == ids).astype(F32).astype(BF16) for pick in picks], axis=0)
        outgoing[span(k * batch, batch), :] = jnp.dot(
            onehot, feat[...], preferred_element_type=F32
        ).astype(BF16)

    slot_at = {
        (dy, dc): rem(y + dy, SIDE) * 2 + rem(core + dc, 2) for dy in range(SIDE) for dc in range(2)
    }

    def send_batch(k, landing, send_sem, recv_sem, with_self=False):
        squares = [square_of(k, a, 1) for a in (0, 1)]
        bases = [pl.multiple_of(k * batch + a * half_batch, half_batch) for a in (0, 1)]
        for dc in (0, 1):
            for dy in (2, 3, 0, 1):
                for a in (0, 1):
                    if with_self and (a, dy, dc) == (0, 0, 0):
                        continue
                    slot = slot_at[dy, dc]
                    pltpu.make_async_remote_copy(
                        src_ref=outgoing.at[span(bases[a] + slot * slots, slots)],
                        dst_ref=landing.at[span(bases[a] + my_slot * slots, slots)],
                        send_sem=send_sem.at[k],
                        recv_sem=recv_sem.at[k],
                        device_id=device(squares[a], slot),
                        device_id_type=MESH,
                    ).start()

    def send_first(landing, send_sem, recv_sem):
        send_batch(0, landing, send_sem, recv_sem, True)
        mine = span(my_slot * slots, slots)
        landing[mine, :] = outgoing[mine, :]

    loads[0].wait()
    gather(0)
    pl.semaphore_wait(barrier, DEVICES - 1)
    send_first(arrived, send1, recv1)

    @pl.loop(1, BATCHES)
    def _(k):
        gather(k)
        send_batch(k, arrived, send1, recv1)

    keys = tile_rows[...] * cols_all + tile_cols[...]
    column = jnp.broadcast_to(keys, (EDGE, count)).T
    tile_ids = lax.broadcasted_iota(jnp.int32, (count, EDGE), 0)
    lanes = lax.broadcasted_iota(jnp.int32, (1, EDGE), 1)

    def last_of(hit):
        found = jnp.max(jnp.where(hit, tile_ids, -1), axis=0, keepdims=True)
        return jnp.where(found < 0, count, found)

    for r in range(row_blocks):
        plan_v[r : r + 1, :] = last_of((column == r * cols_all + lanes) & (lanes < cols_all))
    for h in range(count // EDGE):
        own = keys[:, h * EDGE : (h + 1) * EDGE]
        plan_v[row_blocks + h : row_blocks + h + 1, :] = last_of(
            (column == own) & (tile_ids < lanes + h * EDGE)
        )
    save_plan = pltpu.make_async_copy(plan_v, plan, save_sem)
    save_plan.start()
    save_plan.wait()

    for empty in (tiles, rest, flipped):
        empty[count] = jnp.zeros((EDGE, EDGE), BF16)
    loads[1].wait()

    unroll = 4
    for h in range(count // EDGE):

        @pl.loop(0, EDGE // unroll)
        def _(i):
            for u in range(unroll):
                t = h * EDGE + i * unroll + u
                before = plan[row_blocks + h, i * unroll + u]
                exact = tiles[t].astype(F32) + (tiles[before].astype(F32) + rest[before].astype(F32))
                merged = exact.astype(BF16)
                rest[t] = (exact - merged.astype(F32)).astype(BF16)
                tiles[t] = merged

    @pl.loop(0, count // 8)
    def _(i):
        for u in range(8):
            flipped[i * 8 + u] = tiles[i * 8 + u].T

    lane = lax.broadcasted_iota(jnp.int32, (SQUARES, EDGE), 1) // slots
    per = EDGE // slots
    for h in range(SQUARE // per):
        line = jnp.full((SQUARES, EDGE), -1, jnp.int32)
        for j in range(per):
            row = lst[pl.ds(h * per + j, SQUARES, stride=SQUARE), :]
            line = jnp.where(lane == j, pltpu.roll(row, j * slots, 1) if j else row, line)
        rowtab[:, h * EDGE : (h + 1) * EDGE] = line

    def remote_cols(k, sign):
        per_square = half_batch // EDGE
        first = [row_blocks + square_of(k, a, sign) * per_square for a in (0, 1)]
        return [f + n for f in first for n in range(per_square)]

    def left_of(cols, m):
        bands = [
            jnp.concatenate([tiles[plan[m * wide + r, c]] for c in cols], axis=1) for r in range(wide)
        ]
        return jnp.concatenate(bands, axis=0)

    @pl.loop(0, row_blocks // wide)
    def _(m):
        acc[span(m * batch, batch), :] = jnp.dot(
            left_of(range(row_blocks), m), feat[...], preferred_element_type=F32
        )

    def take(cols, source):
        @pl.loop(0, row_blocks // wide)
        def _(m):
            acc[span(m * batch, batch), :] += jnp.dot(left_of(cols, m), source, preferred_element_type=F32)

    wait_rows(arrived, batch - slots, recv1.at[0])
    take(remote_cols(0, -1), arrived[span(0, batch), :])

    @pl.loop(0, (BATCHES - 2) // 2)
    def _(i):
        k = 1 + 2 * i
        for n in (0, 1):
            wait_rows(arrived, batch, recv1.at[k + n])
        take(remote_cols(k, -1) + remote_cols(k + 1, -1), arrived[pl.ds(pl.multiple_of(k * batch, batch), 2 * batch), :])

    loads[2].wait()
    loads[3].wait()
    last = BATCHES - 1
    wait_rows(arrived, batch, recv1.at[last])
    cols = remote_cols(last, -1)
    source = arrived[span(last * batch, batch), :]
    for b in range(rows_own // batch):
        at = pl.ds(b * batch, batch)
        h = (acc[at, :] + jnp.dot(left_of(cols, b), source, preferred_element_type=F32)).astype(BF16)
        hid[at, :] = h
        pre = jnp.dot(h, wbuf[...], preferred_element_type=F32)
        gate = jax.nn.sigmoid(pre)
        s = (cot[at, :].astype(F32) * gate * (1.0 + pre * (1.0 - gate))).astype(BF16)
        cot[at, :] = (pre * gate).astype(BF16)
        slope[at, :] = s
        hgrad[at, :] = lax.dot_general(
            s, wbuf[...], (((1,), (1,)), ((), ())), preferred_element_type=F32
        ).astype(BF16)

    save_act = pltpu.make_async_copy(cot, activated, save_sem)
    save_act.start()

    def spread(cols):
        bands = [
            jnp.concatenate([flipped[plan[r, c]] for r in range(row_blocks)], axis=1) for c in cols
        ]
        return jnp.dot(jnp.concatenate(bands, axis=0), hgrad[...], preferred_element_type=F32)

    def give(k):
        outgoing[span(k * batch, batch), :] = spread(remote_cols(k, 1)).astype(BF16)

    wait_rows(outgoing, batch - slots, send1.at[0])
    give(0)
    send_first(returned, send2, recv2)

    part[...] = jnp.zeros_like(part)

    @pl.loop(0, rows_own // batch)
    def _(b):
        at = span(b * batch, batch)
        part[...] += lax.dot_general(
            hid[at, :], slope[at, :], (((0,), (0,)), ((), ())), preferred_element_type=F32
        )

    half = width // 2
    mine, other = pl.multiple_of(core * half, half), pl.multiple_of((1 - core) * half, half)
    chips = DEVICES // 2
    chip = div(me, 2)
    square = div(me, SQUARE)
    edge_r, edge_c = chunks.shape[1:]
    across = width // edge_c
    sibling = device(square, y * 2 + 1 - core)
    swap = pltpu.make_async_remote_copy(
        src_ref=part.at[pl.ds(other, half)],
        dst_ref=sib,
        send_sem=sib_send.at[0],
        recv_sem=sib_recv.at[0],
        device_id=sibling,
        device_id_type=MESH,
    )
    swap.start()

    wait_rows(outgoing, batch, send1.at[1])
    give(1)
    send_batch(1, returned, send2, recv2)
    swap.wait()
    wsum[...] = (part[pl.ds(mine, half), :] + sib[...]).astype(BF16)

    def spot(q):
        return div(q, across) * edge_r, rem(q, across) * edge_c

    def mate(q):
        return device(div(q, SIDE), rem(q, SIDE) * 2 + core)

    @pl.loop(1, chips)
    def _(k):
        q = rem(chip + k, chips)
        r0, c0 = spot(q)
        pltpu.make_async_remote_copy(
            src_ref=wsum.at[span(r0, edge_r), span(c0, edge_c)],
            dst_ref=chunks.at[chip],
            send_sem=rs_send,
            recv_sem=rs_recv,
            device_id=mate(q),
            device_id_type=MESH,
        ).start()

    r0, c0 = spot(chip)
    chunks[chip] = wsum[span(r0, edge_r), span(c0, edge_c)]

    def give_batch(k):
        wait_rows(outgoing, batch, send1.at[k])
        give(k)
        send_batch(k, returned, send2, recv2)

    @pl.loop(2, BATCHES)
    def _(k):
        give_batch(k)

    @pl.loop(0, row_blocks // wide)
    def _(n):
        acc[span(n * batch, batch), :] = spread([n * wide + j for j in range(wide)])

    wait_rows(chunks, chips - 1, rs_send)
    wait_rows(chunks, chips - 1, rs_recv)
    gathered[...] = jnp.sum(chunks[...].astype(F32), axis=0).astype(BF16)
    there = (span(mine + r0, edge_r), span(c0, edge_c))
    wall[there[0], there[1]] = gathered[...]

    @pl.loop(1, chips)
    def _(k):
        pltpu.make_async_remote_copy(
            src_ref=gathered,
            dst_ref=wall.at[there[0], there[1]],
            send_sem=ag_send,
            recv_sem=ag_recv,
            device_id=mate(rem(chip + k, chips)),
            device_id_type=MESH,
        ).start()


    tall = 1024

    def picks_of(k):
        return jnp.concatenate([rowtab[pl.ds(square_of(k, a, -1), 1), :] for a in (0, 1)], axis=1)

    def hits(picks, rows, b):
        ids = lax.broadcasted_iota(jnp.int32, (tall, batch), 0) + b * tall
        onehot = (ids == picks).astype(F32).astype(BF16)
        return jnp.dot(onehot, rows, preferred_element_type=F32)

    def add_batch(k):
        picks, rows = picks_of(k), returned[span(k * batch, batch), :]

        @pl.loop(0, rows_own // tall)
        def _(b):
            acc[span(b * tall, tall), :] += hits(picks, rows, b)

    def take_back(k):
        wait_rows(returned, batch, recv2.at[k])
        add_batch(k)

    wait_rows(returned, batch - slots, recv2.at[0])
    add_batch(0)

    @pl.loop(1, last - 1)
    def _(k):
        take_back(k)

    wait_rows(chunks, chips - 1, ag_send)
    wait_rows(chunks, chips - 1, ag_recv)
    back = pltpu.make_async_remote_copy(
        src_ref=wall.at[pl.ds(mine, half)],
        dst_ref=wall.at[pl.ds(mine, half)],
        send_sem=sib_send.at[1],
        recv_sem=sib_recv.at[1],
        device_id=sibling,
        device_id_type=MESH,
    )
    back.start()

    @pl.loop(last - 1, last)
    def _(k):
        take_back(k)

    back.wait()
    save_wall = pltpu.make_async_copy(wall, wgrad, save_sem)
    save_act.wait()
    save_wall.start()
    wait_rows(returned, batch, recv2.at[last])
    picks, rows = picks_of(last), returned[span(last * batch, batch), :]
    saves = []
    for b in range(rows_own // tall):
        at = pl.ds(b * tall, tall)
        hid[at, :] = (acc[at, :] + hits(picks, rows, b)).astype(BF16)
        saves.append(pltpu.make_async_copy(hid.at[at], grad.at[at], load_sem.at[b]))
        saves[-1].start()
    wait_rows(returned, batch - slots, send2.at[0])

    @pl.loop(1, BATCHES)
    def _(k):
        wait_rows(returned, batch, send2.at[k])

    for save in saves:
        save.wait()
    save_wall.wait()


def deliver_kernel(act_in, grad_in, wgrad_in, act_out, grad_out, wgrad_out, act, grad, small, wide, load_sem, save_sem):
    loads, saves = [], []
    for n, (src, via, dst) in enumerate(((act_in, act, act_out), (grad_in, grad, grad_out))):
        rows = src.shape[0] // PARTS
        for p in range(PARTS):
            at = pl.ds(p * rows, rows)
            loads.append(pltpu.make_async_copy(src.at[at], via.at[at], load_sem.at[n, p]))
            saves.append(pltpu.make_async_copy(via.at[at], dst.at[at], save_sem.at[n, p]))
    load_small = pltpu.make_async_copy(wgrad_in, small, load_sem.at[2, 0])
    save_wide = pltpu.make_async_copy(wide, wgrad_out, save_sem.at[2, 0])
    load_small.start()
    for load in loads:
        load.start()
    load_small.wait()
    wide[...] = small[...].astype(F32)
    save_wide.start()
    for load, save in zip(loads, saves):
        load.wait()
        save.start()
    for save in saves:
        save.wait()
    save_wide.wait()


def per_device(features, weight, cotangent, tile_vals, tile_rows, tile_cols, send_rows, counts):
    rows_own, width = features.shape
    count = tile_vals.shape[0]
    slots = send_rows.shape[2]
    row_blocks = rows_own // EDGE
    remote_rows = DEVICES * slots
    cols_all = row_blocks + remote_rows // EDGE
    batch = 2 * SQUARE * slots

    any_ = pl.BlockSpec(memory_space=pl.ANY)
    vmem = pl.BlockSpec(memory_space=pltpu.VMEM)
    chips = DEVICES // 2
    edge_r = width * width // 2 // chips // EDGE
    dma = pltpu.SemaphoreType.DMA
    rows16 = pltpu.VMEM((rows_own, width), BF16)
    far16 = pltpu.VMEM((remote_rows, width), BF16)
    activated, grad, weight_grad = pl.pallas_call(
        network_kernel,
        out_shape=(
            jax.ShapeDtypeStruct((rows_own, width), BF16),
            jax.ShapeDtypeStruct((rows_own, width), BF16),
            jax.ShapeDtypeStruct((width, width), BF16),
        ),
        in_specs=[vmem] * 4 + [any_] * 4,
        out_specs=(any_,) * 3,
        scratch_shapes=[
            pltpu.VMEM((24, EDGE), jnp.int32),
            pltpu.SMEM((24, EDGE), jnp.int32),
            rows16,
            pltpu.VMEM((count + 1, EDGE, EDGE), BF16),
            pltpu.VMEM((count + 1, EDGE, EDGE), BF16),
            pltpu.VMEM((count + 1, EDGE, EDGE), BF16),
            pltpu.VMEM((width, width), BF16),
            rows16,
            pltpu.VMEM((DEVICES, EDGE), jnp.int32),
            pltpu.VMEM((SQUARES, SQUARE * slots), jnp.int32),
            far16,
            far16,
            pltpu.VMEM((rows_own, width), F32),
            rows16,
            rows16,
            rows16,
            far16,
            pltpu.VMEM((width, width), F32),
            pltpu.VMEM((width // 2, width), BF16),
            pltpu.VMEM((width // 2, width), F32),
            pltpu.VMEM((chips, edge_r, EDGE), BF16),
            pltpu.VMEM((edge_r, EDGE), BF16),
            pltpu.VMEM((width, width), BF16),
            dma((4,)),
            dma,
            dma((BATCHES,)),
            dma((BATCHES,)),
            dma((BATCHES,)),
            dma((BATCHES,)),
            dma((2,)),
            dma((2,)),
            dma,
            dma,
            dma,
            dma,
        ],
        compiler_params=pltpu.CompilerParams(
            collective_id=0, has_side_effects=True, vmem_limit_bytes=VMEM_LIMIT
        ),
        name="network",
    )(send_rows[0].T, counts, tile_rows.reshape(1, count), tile_cols.reshape(1, count), features, tile_vals, weight, cotangent)
    return pl.pallas_call(
        deliver_kernel,
        out_shape=(
            jax.ShapeDtypeStruct((rows_own, width), BF16),
            jax.ShapeDtypeStruct((rows_own, width), BF16),
            jax.ShapeDtypeStruct((width, width), F32),
        ),
        in_specs=[any_] * 3,
        out_specs=(any_,) * 3,
        scratch_shapes=[
            rows16,
            rows16,
            pltpu.VMEM((width, width), BF16),
            pltpu.VMEM((width, width), F32),
            dma((3, PARTS)),
            dma((3, PARTS)),
        ],
        compiler_params=pltpu.CompilerParams(vmem_limit_bytes=VMEM_LIMIT),
        name="deliver",
    )(activated, grad, weight_grad)


def solution(mesh):
    rows = P(("group", "local"), None)
    tiles = P(("group", "local"), None, None)
    flat = P(("group", "local"))
    return jax.shard_map(
        per_device,
        mesh=mesh,
        in_specs=(rows, P(), rows, tiles, flat, flat, tiles, rows),
        out_specs=(rows, rows, P()),
        check_vma=False,
    )
```

```python
import functools

import jax
import jax.numpy as jnp
from jax import lax
from jax.experimental import pallas as pl
from jax.experimental.pallas import tpu as pltpu
from jax.sharding import PartitionSpec as P

MESH = pl.DeviceIdType.MESH
F32 = jnp.float32
BF16 = jnp.bfloat16
VMEM_LIMIT = 60 * 1024 * 1024
EDGE = 128
SIDE = 4
SQUARE = 8
SQUARES = SIDE * SIDE
DEVICES = SQUARES * SQUARE
BATCHES = SQUARES // 2
PARTS = 4


def div(a, b):
    return a // b if isinstance(a, int) else lax.div(a, b)


def rem(a, b):
    return a % b if isinstance(a, int) else lax.rem(a, b)


def span(at, size):
    return pl.ds(pl.multiple_of(at, size), size)


def wait_rows(ref, rows, sem):
    view = ref.at[pl.ds(0, rows)]
    pltpu.make_async_copy(view, view, sem).wait()


def network_kernel(
    lists, live, tile_rows, tile_cols, feat_in, vals, weight_in, cot_in,
    activated, grad, wgrad,
    plan_v, plan, feat, tiles, rest, flipped, wbuf, cot, lst, rowtab, outgoing, arrived, acc, hid, slope, hgrad,
    returned, part, wsum, sib, chunks, gathered, wall,
    load_sem, save_sem, send1, recv1, send2, recv2, sib_send, sib_recv, rs_send, rs_recv, ag_send, ag_recv,
):
    me = lax.axis_index("group") * (2 * SQUARE) + lax.axis_index("local")
    z, x = div(me, SIDE * SQUARE), rem(div(me, SQUARE), SIDE)
    y, core = rem(div(me, 2), SIDE), rem(me, 2)
    my_slot = y * 2 + core
    count = vals.shape[0]
    rows_own, width = feat.shape
    slots = lists.shape[0]
    row_blocks = rows_own // EDGE
    cols_all = row_blocks + DEVICES * slots // EDGE
    half_batch = SQUARE * slots
    batch = 2 * half_batch
    wide = batch // EDGE

    def device(square, slot):
        return (div(square, 2), rem(square, 2) * SQUARE + slot)

    def square_of(k, a, sign):
        dz, dx = div(k, SIDE) + 2 * a, rem(k, SIDE) + 2 * a
        return rem(z + SIDE + sign * dz, SIDE) * SIDE + rem(x + 2 * SIDE + sign * dx, SIDE)

    loads = [
        pltpu.make_async_copy(feat_in, feat, load_sem.at[0]),
        pltpu.make_async_copy(vals, tiles.at[pl.ds(0, count)], load_sem.at[1]),
        pltpu.make_async_copy(cot_in, cot, load_sem.at[2]),
        pltpu.make_async_copy(weight_in, wbuf, load_sem.at[3]),
    ]
    for load in loads:
        load.start()

    barrier = pltpu.get_barrier_semaphore()

    def greet(square, slot):
        pl.semaphore_signal(barrier, inc=1, device_id=device(square, slot), device_id_type=MESH)

    my_square = div(me, SQUARE)
    for j in range(1, SQUARE):
        greet(my_square, rem(my_slot + j, SQUARE))

    @pl.loop(1, SQUARES)
    def _(k):
        square = rem(my_square + k, SQUARES)
        for j in range(SQUARE):
            greet(square, j)

    rank = lax.broadcasted_iota(jnp.int32, (slots, DEVICES), 0)
    masked = jnp.where(rank < live[...], lists[...], -1)
    lst[...] = jnp.concatenate([masked, jnp.full((EDGE - slots, DEVICES), -1, jnp.int32)], axis=0).T

    def gather(k):
        picks = []
        for a in (0, 1):
            columns = lst[span(square_of(k, a, 1) * SQUARE, SQUARE), :].T
            picks += [columns[:slots, j : j + 1] for j in range(SQUARE)]
        ids = lax.broadcasted_iota(jnp.int32, (slots, rows_own), 1)
        onehot = jnp.concatenate([(pick == ids).astype(F32).astype(BF16) for pick in picks], axis=0)
        outgoing[span(k * batch, batch), :] = jnp.dot(
            onehot, feat[...], preferred_element_type=F32
        ).astype(BF16)

    slot_at = {
        (dy, dc): rem(y + dy, SIDE) * 2 + rem(core + dc, 2) for dy in range(SIDE) for dc in range(2)
    }

    def send_batch(k, landing, send_sem, recv_sem, with_self=False):
        squares = [square_of(k, a, 1) for a in (0, 1)]
        bases = [pl.multiple_of(k * batch + a * half_batch, half_batch) for a in (0, 1)]
        for dc in (0, 1):
            for dy in (2, 3, 0, 1):
                for a in (0, 1):
                    if with_self and (a, dy, dc) == (0, 0, 0):
                        continue
                    slot = slot_at[dy, dc]
                    pltpu.make_async_remote_copy(
                        src_ref=outgoing.at[span(bases[a] + slot * slots, slots)],
                        dst_ref=landing.at[span(bases[a] + my_slot * slots, slots)],
                        send_sem=send_sem.at[k],
                        recv_sem=recv_sem.at[k],
                        device_id=device(squares[a], slot),
                        device_id_type=MESH,
                    ).start()

    def send_first(landing, send_sem, recv_sem):
        send_batch(0, landing, send_sem, recv_sem, True)
        mine = span(my_slot * slots, slots)
        landing[mine, :] = outgoing[mine, :]

    loads[0].wait()
    gather(0)
    pl.semaphore_wait(barrier, DEVICES - 1)
    send_first(arrived, send1, recv1)

    @pl.loop(1, BATCHES)
    def _(k):
        gather(k)
        send_batch(k, arrived, send1, recv1)

    keys = tile_rows[...] * cols_all + tile_cols[...]
    column = jnp.broadcast_to(keys, (EDGE, count)).T
    tile_ids = lax.broadcasted_iota(jnp.int32, (count, EDGE), 0)
    lanes = lax.broadcasted_iota(jnp.int32, (1, EDGE), 1)

    def last_of(hit):
        found = jnp.max(jnp.where(hit, tile_ids, -1), axis=0, keepdims=True)
        return jnp.where(found < 0, count, found)

    for r in range(row_blocks):
        plan_v[r : r + 1, :] = last_of((column == r * cols_all + lanes) & (lanes < cols_all))
    for h in range(count // EDGE):
        own = keys[:, h * EDGE : (h + 1) * EDGE]
        plan_v[row_blocks + h : row_blocks + h + 1, :] = last_of(
            (column == own) & (tile_ids < lanes + h * EDGE)
        )
    save_plan = pltpu.make_async_copy(plan_v, plan, save_sem)
    save_plan.start()
    save_plan.wait()

    for empty in (tiles, rest, flipped):
        empty[count] = jnp.zeros((EDGE, EDGE), BF16)
    loads[1].wait()

    unroll = 4
    for h in range(count // EDGE):

        @pl.loop(0, EDGE // unroll)
        def _(i):
            for u in range(unroll):
                t = h * EDGE + i * unroll + u
                before = plan[row_blocks + h, i * unroll + u]
                exact = tiles[t].astype(F32) + (tiles[before].astype(F32) + rest[before].astype(F32))
                merged = exact.astype(BF16)
                rest[t] = (exact - merged.astype(F32)).astype(BF16)
                tiles[t] = merged

    @pl.loop(0, count // 8)
    def _(i):
        for u in range(8):
            flipped[i * 8 + u] = tiles[i * 8 + u].T

    lane = lax.broadcasted_iota(jnp.int32, (SQUARES, EDGE), 1) // slots
    per = EDGE // slots
    for h in range(SQUARE // per):
        line = jnp.full((SQUARES, EDGE), -1, jnp.int32)
        for j in range(per):
            row = lst[pl.ds(h * per + j, SQUARES, stride=SQUARE), :]
            line = jnp.where(lane == j, pltpu.roll(row, j * slots, 1) if j else row, line)
        rowtab[:, h * EDGE : (h + 1) * EDGE] = line

    def remote_cols(k, sign):
        per_square = half_batch // EDGE
        first = [row_blocks + square_of(k, a, sign) * per_square for a in (0, 1)]
        return [f + n for f in first for n in range(per_square)]

    def left_of(cols, m):
        bands = [
            jnp.concatenate([tiles[plan[m * wide + r, c]] for c in cols], axis=1) for r in range(wide)
        ]
        return jnp.concatenate(bands, axis=0)

    @pl.loop(0, row_blocks // wide)
    def _(m):
        acc[span(m * batch, batch), :] = jnp.dot(
            left_of(range(row_blocks), m), feat[...], preferred_element_type=F32
        )

    def take(cols, source):
        @pl.loop(0, row_blocks // wide)
        def _(m):
            acc[span(m * batch, batch), :] += jnp.dot(left_of(cols, m), source, preferred_element_type=F32)

    wait_rows(arrived, batch - slots, recv1.at[0])
    take(remote_cols(0, -1), arrived[span(0, batch), :])

    @pl.loop(0, (BATCHES - 2) // 2)
    def _(i):
        k = 1 + 2 * i
        for n in (0, 1):
            wait_rows(arrived, batch, recv1.at[k + n])
        take(remote_cols(k, -1) + remote_cols(k + 1, -1), arrived[pl.ds(pl.multiple_of(k * batch, batch), 2 * batch), :])

    loads[2].wait()
    loads[3].wait()
    last = BATCHES - 1
    wait_rows(arrived, batch, recv1.at[last])
    cols = remote_cols(last, -1)
    source = arrived[span(last * batch, batch), :]
    for b in range(rows_own // batch):
        at = pl.ds(b * batch, batch)
        h = (acc[at, :] + jnp.dot(left_of(cols, b), source, preferred_element_type=F32)).astype(BF16)
        hid[at, :] = h
        pre = jnp.dot(h, wbuf[...], preferred_element_type=F32)
        gate = jax.nn.sigmoid(pre)
        s = (cot[at, :].astype(F32) * gate * (1.0 + pre * (1.0 - gate))).astype(BF16)
        cot[at, :] = (pre * gate).astype(BF16)
        slope[at, :] = s
        hgrad[at, :] = lax.dot_general(
            s, wbuf[...], (((1,), (1,)), ((), ())), preferred_element_type=F32
        ).astype(BF16)

    save_act = pltpu.make_async_copy(cot, activated, save_sem)
    save_act.start()

    def spread(cols):
        bands = [
            jnp.concatenate([flipped[plan[r, c]] for r in range(row_blocks)], axis=1) for c in cols
        ]
        return jnp.dot(jnp.concatenate(bands, axis=0), hgrad[...], preferred_element_type=F32)

    def give(k):
        outgoing[span(k * batch, batch), :] = spread(remote_cols(k, 1)).astype(BF16)

    wait_rows(outgoing, batch - slots, send1.at[0])
    give(0)
    send_first(returned, send2, recv2)

    part[...] = jnp.zeros_like(part)

    @pl.loop(0, rows_own // batch)
    def _(b):
        at = span(b * batch, batch)
        part[...] += lax.dot_general(
            hid[at, :], slope[at, :], (((0,), (0,)), ((), ())), preferred_element_type=F32
        )

    half = width // 2
    mine, other = pl.multiple_of(core * half, half), pl.multiple_of((1 - core) * half, half)
    chips = DEVICES // 2
    chip = div(me, 2)
    square = div(me, SQUARE)
    edge_r, edge_c = chunks.shape[1:]
    across = width // edge_c
    sibling = device(square, y * 2 + 1 - core)
    swap = pltpu.make_async_remote_copy(
        src_ref=part.at[pl.ds(other, half)],
        dst_ref=sib,
        send_sem=sib_send.at[0],
        recv_sem=sib_recv.at[0],
        device_id=sibling,
        device_id_type=MESH,
    )
    swap.start()

    wait_rows(outgoing, batch, send1.at[1])
    give(1)
    send_batch(1, returned, send2, recv2)
    swap.wait()
    wsum[...] = (part[pl.ds(mine, half), :] + sib[...]).astype(BF16)

    def spot(q):
        return div(q, across) * edge_r, rem(q, across) * edge_c

    def mate(q):
        return device(div(q, SIDE), rem(q, SIDE) * 2 + core)

    def to_mates(put):
        def squares(k, skip):
            for dy in (2, 3, 0, 1):
                for a in (0, 1):
                    if not (skip and (a, dy) == (0, 0)):
                        put(square_of(k, a, 1) * SIDE + rem(y + dy, SIDE))

        squares(0, True)

        @pl.loop(1, BATCHES)
        def _(k):
            squares(k, False)

    def scatter_part(q):
        r0, c0 = spot(q)
        pltpu.make_async_remote_copy(
            src_ref=wsum.at[span(r0, edge_r), span(c0, edge_c)],
            dst_ref=chunks.at[chip],
            send_sem=rs_send,
            recv_sem=rs_recv,
            device_id=mate(q),
            device_id_type=MESH,
        ).start()

    to_mates(scatter_part)
    r0, c0 = spot(chip)
    chunks[chip] = wsum[span(r0, edge_r), span(c0, edge_c)]

    def give_batch(k):
        wait_rows(outgoing, batch, send1.at[k])
        give(k)
        send_batch(k, returned, send2, recv2)

    @pl.loop(2, BATCHES - 2)
    def _(k):
        give_batch(k)

    @pl.loop(0, row_blocks // wide)
    def _(n):
        acc[span(n * batch, batch), :] = spread([n * wide + j for j in range(wide)])

    wait_rows(chunks, chips - 1, rs_send)
    wait_rows(chunks, chips - 1, rs_recv)
    gathered[...] = jnp.sum(chunks[...].astype(F32), axis=0).astype(BF16)
    there = (span(mine + r0, edge_r), span(c0, edge_c))
    wall[there[0], there[1]] = gathered[...]

    def share_sum(q):
        pltpu.make_async_remote_copy(
            src_ref=gathered,
            dst_ref=wall.at[there[0], there[1]],
            send_sem=ag_send,
            recv_sem=ag_recv,
            device_id=mate(q),
            device_id_type=MESH,
        ).start()

    to_mates(share_sum)

    @pl.loop(BATCHES - 2, BATCHES)
    def _(k):
        give_batch(k)

    tall = 1024

    def picks_of(k):
        return jnp.concatenate([rowtab[pl.ds(square_of(k, a, -1), 1), :] for a in (0, 1)], axis=1)

    def hits(picks, rows, b):
        ids = lax.broadcasted_iota(jnp.int32, (tall, batch), 0) + b * tall
        onehot = (ids == picks).astype(F32).astype(BF16)
        return jnp.dot(onehot, rows, preferred_element_type=F32)

    def add_batch(k):
        picks, rows = picks_of(k), returned[span(k * batch, batch), :]

        @pl.loop(0, rows_own // tall)
        def _(b):
            acc[span(b * tall, tall), :] += hits(picks, rows, b)

    def take_back(k):
        wait_rows(returned, batch, recv2.at[k])
        add_batch(k)

    wait_rows(returned, batch - slots, recv2.at[0])
    add_batch(0)

    @pl.loop(1, last - 1)
    def _(k):
        take_back(k)

    wait_rows(chunks, chips - 1, ag_send)
    wait_rows(chunks, chips - 1, ag_recv)
    back = pltpu.make_async_remote_copy(
        src_ref=wall.at[pl.ds(mine, half)],
        dst_ref=wall.at[pl.ds(mine, half)],
        send_sem=sib_send.at[1],
        recv_sem=sib_recv.at[1],
        device_id=sibling,
        device_id_type=MESH,
    )
    back.start()

    @pl.loop(last - 1, last)
    def _(k):
        take_back(k)

    back.wait()
    save_wall = pltpu.make_async_copy(wall, wgrad, save_sem)
    save_act.wait()
    save_wall.start()
    wait_rows(returned, batch, recv2.at[last])
    picks, rows = picks_of(last), returned[span(last * batch, batch), :]
    saves = []
    for b in range(rows_own // tall):
        at = pl.ds(b * tall, tall)
        hid[at, :] = (acc[at, :] + hits(picks, rows, b)).astype(BF16)
        saves.append(pltpu.make_async_copy(hid.at[at], grad.at[at], load_sem.at[b]))
        saves[-1].start()
    wait_rows(returned, batch - slots, send2.at[0])

    @pl.loop(1, BATCHES)
    def _(k):
        wait_rows(returned, batch, send2.at[k])

    for save in saves:
        save.wait()
    save_wall.wait()


def deliver_kernel(act_in, grad_in, wgrad_in, act_out, grad_out, wgrad_out, act, grad, small, wide, load_sem, save_sem):
    loads, saves = [], []
    for n, (src, via, dst) in enumerate(((act_in, act, act_out), (grad_in, grad, grad_out))):
        rows = src.shape[0] // PARTS
        for p in range(PARTS):
            at = pl.ds(p * rows, rows)
            loads.append(pltpu.make_async_copy(src.at[at], via.at[at], load_sem.at[n, p]))
            saves.append(pltpu.make_async_copy(via.at[at], dst.at[at], save_sem.at[n, p]))
    load_small = pltpu.make_async_copy(wgrad_in, small, load_sem.at[2, 0])
    save_wide = pltpu.make_async_copy(wide, wgrad_out, save_sem.at[2, 0])
    load_small.start()
    for load in loads:
        load.start()
    load_small.wait()
    wide[...] = small[...].astype(F32)
    save_wide.start()
    for load, save in zip(loads, saves):
        load.wait()
        save.start()
    for save in saves:
        save.wait()
    save_wide.wait()


def per_device(features, weight, cotangent, tile_vals, tile_rows, tile_cols, send_rows, counts):
    rows_own, width = features.shape
    count = tile_vals.shape[0]
    slots = send_rows.shape[2]
    row_blocks = rows_own // EDGE
    remote_rows = DEVICES * slots
    cols_all = row_blocks + remote_rows // EDGE
    batch = 2 * SQUARE * slots

    any_ = pl.BlockSpec(memory_space=pl.ANY)
    vmem = pl.BlockSpec(memory_space=pltpu.VMEM)
    chips = DEVICES // 2
    edge_r = width * width // 2 // chips // EDGE
    dma = pltpu.SemaphoreType.DMA
    rows16 = pltpu.VMEM((rows_own, width), BF16)
    far16 = pltpu.VMEM((remote_rows, width), BF16)
    activated, grad, weight_grad = pl.pallas_call(
        network_kernel,
        out_shape=(
            jax.ShapeDtypeStruct((rows_own, width), BF16),
            jax.ShapeDtypeStruct((rows_own, width), BF16),
            jax.ShapeDtypeStruct((width, width), BF16),
        ),
        in_specs=[vmem] * 4 + [any_] * 4,
        out_specs=(any_,) * 3,
        scratch_shapes=[
            pltpu.VMEM((24, EDGE), jnp.int32),
            pltpu.SMEM((24, EDGE), jnp.int32),
            rows16,
            pltpu.VMEM((count + 1, EDGE, EDGE), BF16),
            pltpu.VMEM((count + 1, EDGE, EDGE), BF16),
            pltpu.VMEM((count + 1, EDGE, EDGE), BF16),
            pltpu.VMEM((width, width), BF16),
            rows16,
            pltpu.VMEM((DEVICES, EDGE), jnp.int32),
            pltpu.VMEM((SQUARES, SQUARE * slots), jnp.int32),
            far16,
            far16,
            pltpu.VMEM((rows_own, width), F32),
            rows16,
            rows16,
            rows16,
            far16,
            pltpu.VMEM((width, width), F32),
            pltpu.VMEM((width // 2, width), BF16),
            pltpu.VMEM((width // 2, width), F32),
            pltpu.VMEM((chips, edge_r, EDGE), BF16),
            pltpu.VMEM((edge_r, EDGE), BF16),
            pltpu.VMEM((width, width), BF16),
            dma((4,)),
            dma,
            dma((BATCHES,)),
            dma((BATCHES,)),
            dma((BATCHES,)),
            dma((BATCHES,)),
            dma((2,)),
            dma((2,)),
            dma,
            dma,
            dma,
            dma,
        ],
        compiler_params=pltpu.CompilerParams(
            collective_id=0, has_side_effects=True, vmem_limit_bytes=VMEM_LIMIT
        ),
        name="network",
    )(send_rows[0].T, counts, tile_rows.reshape(1, count), tile_cols.reshape(1, count), features, tile_vals, weight, cotangent)
    return pl.pallas_call(
        deliver_kernel,
        out_shape=(
            jax.ShapeDtypeStruct((rows_own, width), BF16),
            jax.ShapeDtypeStruct((rows_own, width), BF16),
            jax.ShapeDtypeStruct((width, width), F32),
        ),
        in_specs=[any_] * 3,
        out_specs=(any_,) * 3,
        scratch_shapes=[
            rows16,
            rows16,
            pltpu.VMEM((width, width), BF16),
            pltpu.VMEM((width, width), F32),
            dma((3, PARTS)),
            dma((3, PARTS)),
        ],
        compiler_params=pltpu.CompilerParams(vmem_limit_bytes=VMEM_LIMIT),
        name="deliver",
    )(activated, grad, weight_grad)


def solution(mesh):
    rows = P(("group", "local"), None)
    tiles = P(("group", "local"), None, None)
    flat = P(("group", "local"))
    return jax.shard_map(
        per_device,
        mesh=mesh,
        in_specs=(rows, P(), rows, tiles, flat, flat, tiles, rows),
        out_specs=(rows, rows, P()),
        check_vma=False,
    )
```
